32 devices in a mesh: row: 8 (over z, x), col: 4 (over y, core).
Axes of the slice: x: 2, y: 2, z: 4, core: 2. Of those that a mesh axis runs over, the one named last changes fastest.
Arguments:
- matrix: float32 [3584, 3584], P('row', 'col'), may hold values from -3 to 3
- reflectors: float32 [1, 64, 3584], P(None, None, 'row'), may hold values from -0.1875 to 0.1875
- factors: float32 [1, 64, 64], replicated, may hold values from -0.1 to 2, as said below
Outputs:
- updated: float32 [3584, 3584], P('row', 'col')
- companions: float32 [1, 64, 3584], P(None, None, 'row')
The draws below stay inside these ranges and needn't reach their ends.
Inputs may be any that keep to these rules, and one draw needn't show every extreme that they name: `factors`: each factor is upper triangular (zero below the diagonal) with diagonal entries between 1 and 2.
All inputs are finite; a program needn't handle non-finite values.
Results may differ from the reference program's by a relative error of at most 0.0001.
Values sent between devices are 32-bit elements; how exact they have to be, the bound alone decides.
A program may use at most 64 MiB of HBM per device.

```python
import math
import jax
import jax.numpy as jnp
from jax import lax

B = 64
PANELS = 1
N = 3584


def draw_matrix(key, part):
    first_key = jax.random.fold_in(jax.random.fold_in(key, 11), 0)
    base = jnp.clip(jax.random.normal(first_key, (N, N), jnp.float32), -4.0, 4.0)
    return 0.5 * (base + base.T) / math.sqrt(2.0)


def draw_factors(key, part):
    first_key, second_key = jax.random.split(jax.random.fold_in(key, 23))
    diagonal = jax.random.uniform(first_key, (PANELS, B), jnp.float32, 1.0, 2.0)
    upper = jax.random.uniform(second_key, (PANELS, B, B), jnp.float32, -0.1, 0.1)
    strict = jnp.triu(jnp.ones((B, B), jnp.float32), 1)
    return upper * strict[None, :, :] + diagonal[:, :, None] * jnp.eye(B, dtype=jnp.float32)[None, :, :]


def steps_of(rng, dims, pieces, least, top_value):
    def one(dim, parts):
        steps = jax.random.uniform(jax.random.fold_in(jax.random.fold_in(rng, 6), dim), (parts,), jnp.float32, least / len(pieces), top_value / len(pieces))
        return jnp.repeat(jnp.exp(steps), dims[dim] // parts).reshape((-1,) + (1,) * (len(dims) - dim - 1))

    gain = one(*pieces[0])
    for cut in pieces[1:]:
        gain = gain * one(*cut)
    return gain


def bell_draw(stream_key, shape, scale, most, cuts=(), kind=jnp.bfloat16):
    values = scale * jax.random.normal(stream_key, shape, jnp.float32)
    if cuts:
        values = values * steps_of(stream_key, shape, cuts, -0.22, 0.18)
    return jnp.clip(values, -most, most).astype(kind)


def setup_inputs(seed: int = 0) -> dict:
    streams_of = jax.random.split(jax.random.key(seed), 4)
    matrix = draw_matrix(jax.random.fold_in(streams_of[3], 71), 0)
    reflectors = bell_draw(streams_of[1], (PANELS, B, N), (N // 4) ** -0.5, 0.1875, ((2, 8),), jnp.float32)
    factors = draw_factors(jax.random.fold_in(streams_of[3], 71), 0)
    return {"matrix": matrix, "reflectors": reflectors, "factors": factors}


def contract(left_side, right_side, left_dim, right_dim):
    return lax.dot_general(left_side, right_side, (((left_dim,), (right_dim,)), ((), ())), precision=lax.Precision.HIGHEST, preferred_element_type=jnp.float32)


def reference(matrix, reflectors, factors):
    current = matrix
    results = []
    for step_index in range(PANELS):
        v_rows = reflectors[step_index]
        factor = factors[step_index]
        y_rows = contract(v_rows, current, 1, 1)
        x_rows = contract(factor, y_rows, 0, 0)
        projected = contract(v_rows, x_rows, 1, 1)
        mixing = contract(projected, factor, 0, 0)
        w_rows = x_rows - 0.5 * contract(mixing, v_rows, 1, 0)
        current = current - contract(v_rows, w_rows, 0, 0) - contract(w_rows, v_rows, 0, 0)
        results.append(w_rows)
    return current, jnp.stack(results)
```

```python
import functools

import jax
import jax.numpy as jnp
from jax import lax
from jax.experimental import pallas as pl
from jax.experimental.pallas import tpu as pltpu
from jax.sharding import PartitionSpec as P

MESH = pl.DeviceIdType.MESH


def split(x):
    hi = x.astype(jnp.bfloat16)
    return hi, (x - hi.astype(jnp.float32)).astype(jnp.bfloat16)


def dot(a, b, da, db):
    return lax.dot_general(a, b, (((da,), (db,)), ((), ())), preferred_element_type=jnp.float32)


def dot3(a, b, da, db):
    ah, al = split(a)
    bh, bl = split(b)
    return dot(ah, bh, da, db) + (dot(ah, bl, da, db) + dot(al, bh, da, db))


def kernel(
    nr, nc, v_ref, a_hbm, f_ref, out_ref, w_ref,
    a_ref, a_hi, a_lo, vrecv, pbuf, precv, yown, yrecv, yrow, srow, spart, sown, sfull,
    a_sem, gv_send, gv_recv, rs_send, rs_recv, gy_send, gy_recv, yr_send, yr_recv, sr_send, sr_recv, sc_send, sc_recv,
):
    ratio = nr // nc
    r, c = lax.axis_index("row"), lax.axis_index("col")
    home = r // ratio
    at_home = home == c
    n = v_ref.shape[2]
    b = f_ref.shape[0]
    h = b // nc

    a_copy = pltpu.make_async_copy(a_hbm, a_ref, a_sem)
    a_copy.start()

    def remote(src, dst, send, recv, row, col):
        return pltpu.make_async_remote_copy(
            src_ref=src, dst_ref=dst, send_sem=send, recv_sem=recv, device_id=(row, col), device_id_type=MESH
        )

    row_peers = [lax.rem(r + k, nr) for k in range(1, nr)]
    col_peers = [lax.rem(c + k, nc) for k in range(1, nc)]

    barrier = pltpu.get_barrier_semaphore()
    for t in row_peers:
        pl.semaphore_signal(barrier, inc=1, device_id=(t, c), device_id_type=MESH)
    for q in col_peers:
        pl.semaphore_signal(barrier, inc=1, device_id=(r, q), device_id_type=MESH)
        for i in range(ratio):
            pl.semaphore_signal(barrier, inc=1, device_id=(c * ratio + i, q), device_id_type=MESH)
    pl.semaphore_wait(barrier, nr - 1 + nc - 1 + jnp.where(at_home, 0, nr))

    def gather_copies(src, dst, send, recv):
        return [
            remote(src, dst.at[r % ratio, c], send.at[k], recv.at[r % ratio, c], lax.rem(r + k, nr), home)
            for k in range(nr)
        ]

    def start_gather(src, dst, send, recv):
        copies = gather_copies(src, dst, send, recv)
        for copy in copies[1:]:
            copy.start()

        @pl.when(jnp.logical_not(at_home))
        def _():
            copies[0].start()

        @pl.when(at_home)
        def _():
            dst[r % ratio, c] = src[...]

        return copies

    def wait_gather(src, dst, send, recv):
        for j in range(nc):
            q = lax.rem(c + j, nc)
            for i in range(ratio):
                copy = remote(src, dst.at[i, q], send.at[0], recv.at[i, q], r, c)
                if j == 0:
                    pl.when(c * ratio + i != r)(copy.wait_recv)
                else:
                    copy.wait_recv()

    def end_gather(copies):
        for copy in copies[1:]:
            copy.wait_send()
        pl.when(jnp.logical_not(at_home))(copies[0].wait_send)

    gv = start_gather(v_ref.at[c], vrecv, gv_send, gv_recv)

    a_copy.wait()
    hi, lo = split(a_ref[...])
    a_hi[...] = hi
    a_lo[...] = lo
    v_rows = jnp.concatenate([v_ref[q] for q in range(nc)], axis=0)

    wait_gather(v_ref.at[c], vrecv, gv_send, gv_recv)

    def columns(buf):
        return jnp.concatenate(
            [jnp.concatenate([buf[i, q] for q in range(nc)], axis=0) for i in range(ratio)], axis=1
        )

    v_cols = columns(vrecv)
    vh, vl = split(v_cols)
    both = dot(jnp.concatenate([vh, vl], axis=0), a_hi[...], 1, 1)
    partial = both[:b] + (both[b:] + dot(vh, a_lo[...], 1, 1))
    term = dot3(v_rows, partial, 1, 1)
    for q in range(nc):
        pbuf[q, :, :n] = partial[q * h:(q + 1) * h]
        pbuf[q, :, n:] = term[q * h:(q + 1) * h]

    rs = [remote(pbuf.at[q], precv.at[c], rs_send.at[k], rs_recv.at[c], r, q) for k, q in enumerate(col_peers)]
    for copy in rs:
        copy.start()
    total = pbuf[c]
    for k, q in enumerate(col_peers):
        remote(pbuf.at[q], precv.at[q], rs_send.at[k], rs_recv.at[q], r, q).wait_recv()
        total = total + precv[q]
    yown[...] = total[:, :n]
    spart[...] = total[:, n:]
    srow[r] = total[:, n:]

    sr = [remote(spart, srow.at[r], sr_send.at[k], sr_recv.at[r], t, c) for k, t in enumerate(row_peers)]
    for copy in sr:
        copy.start()
    gy = start_gather(yown, yrecv, gy_send, gy_recv)
    yr = [remote(yown, yrow.at[c], yr_send.at[k], yr_recv.at[c], r, q) for k, q in enumerate(col_peers)]
    for copy in yr:
        copy.start()
    yrow[c] = yown[...]

    for k, t in enumerate(row_peers):
        remote(spart, srow.at[t], sr_send.at[k], sr_recv.at[t], t, c).wait_recv()
    s = srow[0]
    for t in range(1, nr):
        s = s + srow[t]
    sown[...] = s
    sfull[c] = s
    sc = [remote(sown, sfull.at[c], sc_send.at[k], sc_recv.at[c], r, q) for k, q in enumerate(col_peers)]
    for copy in sc:
        copy.start()
    for k, q in enumerate(col_peers):
        remote(sown, sfull.at[q], sc_send.at[k], sc_recv.at[q], r, q).wait_recv()
    square = jnp.concatenate([sfull[q] for q in range(nc)], axis=0)
    factor = f_ref[...]
    mixing = 0.5 * dot3(dot3(square, factor, 1, 0), factor, 0, 0)

    for k, q in enumerate(col_peers):
        remote(yown, yrow.at[q], yr_send.at[k], yr_recv.at[q], r, q).wait_recv()
    y_rows = jnp.concatenate([yrow[q] for q in range(nc)], axis=0)
    w_rows = dot3(factor, y_rows, 0, 0) - dot3(mixing, v_rows, 1, 0)
    w_ref[0] = w_rows

    wait_gather(yown, yrecv, gy_send, gy_recv)
    y_cols = columns(yrecv)
    w_cols = dot3(factor, y_cols, 0, 0) - dot3(mixing, v_cols, 1, 0)

    lh, ll = split(jnp.concatenate([v_rows, w_rows], axis=0))
    rh, rl = split(jnp.concatenate([w_cols, v_cols], axis=0))
    left = jnp.concatenate([lh, lh, ll], axis=0)
    right = jnp.concatenate([rh, rl, rh], axis=0)
    out_ref[...] = a_ref[...] - dot(left, right, 0, 0)

    end_gather(gv)
    end_gather(gy)
    for copy in rs + sr + yr + sc:
        copy.wait_send()


def shards(matrix, reflectors, factors):
    nr, nc = lax.axis_size("row"), lax.axis_size("col")
    _, b, n = reflectors.shape
    m, k = matrix.shape
    ratio, h = nr // nc, b // nc
    f32 = jnp.float32
    dma = pltpu.SemaphoreType.DMA
    vmem = pl.BlockSpec(memory_space=pltpu.VMEM)
    return pl.pallas_call(
        functools.partial(kernel, nr, nc),
        out_shape=(jax.ShapeDtypeStruct((m, k), f32), jax.ShapeDtypeStruct((1, b, n), f32)),
        in_specs=[vmem, pl.BlockSpec(memory_space=pl.ANY), vmem],
        out_specs=(vmem, vmem),
        scratch_shapes=[
            pltpu.VMEM((m, k), f32),
            pltpu.VMEM((m, k), jnp.bfloat16),
            pltpu.VMEM((m, k), jnp.bfloat16),
            pltpu.VMEM((ratio, nc, h, n), f32),
            pltpu.VMEM((nc, h, n + b), f32),
            pltpu.VMEM((nc, h, n + b), f32),
            pltpu.VMEM((h, n), f32),
            pltpu.VMEM((ratio, nc, h, n), f32),
            pltpu.VMEM((nc, h, n), f32),
            pltpu.VMEM((nr, h, b), f32),
            pltpu.VMEM((h, b), f32),
            pltpu.VMEM((h, b), f32),
            pltpu.VMEM((nc, h, b), f32),
            dma(()),
            dma((nr,)), dma((ratio, nc)),
            dma((nc - 1,)), dma((nc,)),
            dma((nr,)), dma((ratio, nc)),
            dma((nc - 1,)), dma((nc,)),
            dma((nr - 1,)), dma((nr,)),
            dma((nc - 1,)), dma((nc,)),
        ],
        compiler_params=pltpu.CompilerParams(
            collective_id=0, has_side_effects=True, vmem_limit_bytes=48 * 1024 * 1024
        ),
        name="reflector_update",
    )(reflectors.reshape(nc, h, n), matrix, factors[0])


def solution(mesh):
    return jax.shard_map(
        shards,
        mesh=mesh,
        in_specs=(P("row", "col"), P(None, None, "row"), P()),
        out_specs=(P("row", "col"), P(None, None, "row")),
        check_vma=False,
    )
```

```python
import functools

import jax
import jax.numpy as jnp
from jax import lax
from jax.experimental import pallas as pl
from jax.experimental.pallas import tpu as pltpu
from jax.sharding import PartitionSpec as P

MESH = pl.DeviceIdType.MESH


def split(x):
    hi = x.astype(jnp.bfloat16)
    return hi, (x - hi.astype(jnp.float32)).astype(jnp.bfloat16)


def dot(a, b, da, db):
    return lax.dot_general(a, b, (((da,), (db,)), ((), ())), preferred_element_type=jnp.float32)


def dot3(a, b, da, db):
    ah, al = split(a)
    bh, bl = split(b)
    return dot(ah, bh, da, db) + (dot(ah, bl, da, db) + dot(al, bh, da, db))


def kernel(
    nr, nc, v_hbm, a_hbm, f_hbm, out_ref, w_ref,
    a_ref, a_hi, a_lo, v_ref, f_ref, vrecv, pbuf, precv, yown, yrecv, yrow, srow, spart, sown, sfull,
    in_sem, gv_send, gv_recv, rs_send, rs_recv, gy_send, gy_recv, yr_send, yr_recv, sr_send, sr_recv, sc_send, sc_recv,
):
    ratio, half = nr // nc, nc // 2
    r, c = lax.axis_index("row"), lax.axis_index("col")
    g, i = r // ratio, r % ratio
    line, core = c // 2, c % 2
    aligned = g % 2 == core
    n = v_ref.shape[2]
    b = f_ref.shape[0]
    h = b // nc

    v_copy = pltpu.make_async_copy(v_hbm, v_ref, in_sem.at[0])
    a_copy = pltpu.make_async_copy(a_hbm, a_ref, in_sem.at[1])
    f_copy = pltpu.make_async_copy(f_hbm, f_ref, in_sem.at[2])
    v_copy.start()
    f_copy.start()
    a_copy.start()

    def remote(src, dst, send, recv, row, col):
        return pltpu.make_async_remote_copy(
            src_ref=src, dst_ref=dst, send_sem=send, recv_sem=recv, device_id=(row, col), device_id_type=MESH
        )

    row_peers = [lax.rem(r + k, nr) for k in range(1, nr)]
    col_peers = [lax.rem(c + k, nc) for k in range(1, nc)]

    def signal(row, col):
        pl.semaphore_signal(barrier, inc=1, device_id=(row, col), device_id_type=MESH)

    barrier = pltpu.get_barrier_semaphore()
    for t in row_peers:
        signal(t, c)
    for q in col_peers:
        signal(r, q)
    for d in range(ratio):
        for e in range(half):
            if d or e:
                signal(g * ratio + lax.rem(i + d, ratio), lax.rem(line + e, half) * 2 + core)
    for j in range(half):
        for e in range(2):
            row = (lax.rem(g // 2 + j, half) * 2 + core) * ratio + i
            col = line * 2 + lax.rem(core + e, 2)
            if j or e:
                signal(row, col)
            else:
                pl.when(jnp.logical_not(aligned))(functools.partial(signal, row, col))
    count = nr - 1 + nc - 1 + ratio * half - 1 + nc
    pl.semaphore_wait(barrier, count - jnp.where(aligned, 1, 0))

    relay = ratio * nc

    class Gather:
        def __init__(self, src, buf, send, recv):
            self.src, self.buf, self.send, self.recv = src, buf, send, recv
            slot = jnp.where(g // 2 == line, i * nc + c, relay + (g // 2) * 2 + core)
            self.first = [
                remote(
                    src, buf.at[slot], send.at[j], recv.at[slot],
                    lax.rem(g + j, nc) * ratio + i, line * 2 + g % 2,
                )
                for j in range(nc)
            ]
            for copy in self.first[1:]:
                copy.start()
            pl.when(jnp.logical_not(aligned))(self.first[0].start)

            @pl.when(aligned)
            def _():
                buf[slot] = src[...]

        def forward(self):
            self.second = []
            k = nc
            for j in list(range(1, half)) + [0]:
                a = lax.rem(line + j, half)
                for e in range(2):
                    final = i * nc + line * 2 + e
                    slot = relay + a * 2 + e if j else final
                    mine = jnp.logical_and(a * 2 + core == g, e == core)
                    arrival = remote(self.src, self.buf.at[slot], self.send.at[0], self.recv.at[slot], r, c)
                    pl.when(jnp.logical_not(mine))(arrival.wait_recv)
                    for d in range(0 if j else 1, ratio):
                        copy = remote(
                            self.buf.at[slot], self.buf.at[final], self.send.at[k], self.recv.at[final],
                            g * ratio + lax.rem(i + d, ratio), a * 2 + core,
                        )
                        copy.start()
                        self.second.append(copy)
                        k += 1

        def wait(self):
            for d in range(ratio):
                for e in range(half):
                    for k in range(2):
                        if d or e:
                            slot = lax.rem(i + d, ratio) * nc + lax.rem(line + e, half) * 2 + k
                            remote(
                                self.src, self.buf.at[slot], self.send.at[0], self.recv.at[slot], r, c
                            ).wait_recv()

        def columns(self):
            return jnp.concatenate(
                [
                    jnp.concatenate([self.buf[t * nc + q] for q in range(nc)], axis=0)
                    for t in range(ratio)
                ],
                axis=1,
            )

        def end(self):
            pl.when(jnp.logical_not(aligned))(self.first[0].wait_send)
            for copy in self.first[1:] + self.second:
                copy.wait_send()

    v_copy.wait()
    gv = Gather(v_ref.at[c], vrecv, gv_send, gv_recv)
    gv.forward()

    f_copy.wait()
    a_copy.wait()
    hi, lo = split(a_ref[...])
    a_hi[...] = hi
    a_lo[...] = lo
    v_rows = jnp.concatenate([v_ref[q] for q in range(nc)], axis=0)

    gv.wait()
    v_cols = gv.columns()
    vh, vl = split(v_cols)
    both = dot(jnp.concatenate([vh, vl], axis=0), a_hi[...], 1, 1)
    partial = both[:b] + (both[b:] + dot(vh, a_lo[...], 1, 1))
    term = dot3(v_rows, partial, 1, 1)
    for q in range(nc):
        pbuf[q, :, :n] = partial[q * h:(q + 1) * h]
        pbuf[q, :, n:] = term[q * h:(q + 1) * h]

    rs = [remote(pbuf.at[q], precv.at[c], rs_send.at[k], rs_recv.at[c], r, q) for k, q in enumerate(col_peers)]
    for copy in rs:
        copy.start()
    total = pbuf[c]
    for k, q in enumerate(col_peers):
        remote(pbuf.at[q], precv.at[q], rs_send.at[k], rs_recv.at[q], r, q).wait_recv()
        total = total + precv[q]
    yown[...] = total[:, :n]
    spart[...] = total[:, n:]
    srow[r] = total[:, n:]

    gy = Gather(yown, yrecv, gy_send, gy_recv)
    sr = [remote(spart, srow.at[r], sr_send.at[k], sr_recv.at[r], t, c) for k, t in enumerate(row_peers)]
    for copy in sr:
        copy.start()
    yr = [remote(yown, yrow.at[c], yr_send.at[k], yr_recv.at[c], r, q) for k, q in enumerate(col_peers)]
    for copy in yr:
        copy.start()
    yrow[c] = yown[...]
    gy.forward()

    for k, t in enumerate(row_peers):
        remote(spart, srow.at[t], sr_send.at[k], sr_recv.at[t], t, c).wait_recv()
    s = srow[0]
    for t in range(1, nr):
        s = s + srow[t]
    sown[...] = s
    sfull[c] = s
    sc = [remote(sown, sfull.at[c], sc_send.at[k], sc_recv.at[c], r, q) for k, q in enumerate(col_peers)]
    for copy in sc:
        copy.start()
    for k, q in enumerate(col_peers):
        remote(sown, sfull.at[q], sc_send.at[k], sc_recv.at[q], r, q).wait_recv()
    square = jnp.concatenate([sfull[q] for q in range(nc)], axis=0)
    factor = f_ref[...]
    mixing = 0.5 * dot3(dot3(square, factor, 1, 0), factor, 0, 0)

    for k, q in enumerate(col_peers):
        remote(yown, yrow.at[q], yr_send.at[k], yr_recv.at[q], r, q).wait_recv()
    y_rows = jnp.concatenate([yrow[q] for q in range(nc)], axis=0)
    w_rows = dot3(factor, y_rows, 0, 0) - dot3(mixing, v_rows, 1, 0)
    w_ref[0] = w_rows

    gy.wait()
    w_cols = dot3(factor, gy.columns(), 0, 0) - dot3(mixing, v_cols, 1, 0)

    lh, ll = split(jnp.concatenate([v_rows, w_rows], axis=0))
    rh, rl = split(jnp.concatenate([w_cols, v_cols], axis=0))
    left = jnp.concatenate([lh, lh, ll], axis=0)
    right = jnp.concatenate([rh, rl, rh], axis=0)
    out_ref[...] = a_ref[...] - dot(left, right, 0, 0)

    gv.end()
    gy.end()
    for copy in rs + sr + yr + sc:
        copy.wait_send()


def shards(matrix, reflectors, factors):
    nr, nc = lax.axis_size("row"), lax.axis_size("col")
    _, b, n = reflectors.shape
    m, k = matrix.shape
    ratio, h = nr // nc, b // nc
    f32 = jnp.float32
    dma = pltpu.SemaphoreType.DMA
    vmem = pl.BlockSpec(memory_space=pltpu.VMEM)
    hbm = pl.BlockSpec(memory_space=pltpu.HBM)
    slots = ratio * nc + nc
    sends = nc + 2 * (ratio * (nc // 2) - 1)
    return pl.pallas_call(
        functools.partial(kernel, nr, nc),
        out_shape=(jax.ShapeDtypeStruct((m, k), f32), jax.ShapeDtypeStruct((1, b, n), f32)),
        in_specs=[hbm, hbm, hbm],
        out_specs=(vmem, vmem),
        scratch_shapes=[
            pltpu.VMEM((m, k), f32),
            pltpu.VMEM((m, k), jnp.bfloat16),
            pltpu.VMEM((m, k), jnp.bfloat16),
            pltpu.VMEM((nc, h, n), f32),
            pltpu.VMEM((b, b), f32),
            pltpu.VMEM((slots, h, n), f32),
            pltpu.VMEM((nc, h, n + b), f32),
            pltpu.VMEM((nc, h, n + b), f32),
            pltpu.VMEM((h, n), f32),
            pltpu.VMEM((slots, h, n), f32),
            pltpu.VMEM((nc, h, n), f32),
            pltpu.VMEM((nr, h, b), f32),
            pltpu.VMEM((h, b), f32),
            pltpu.VMEM((h, b), f32),
            pltpu.VMEM((nc, h, b), f32),
            dma((3,)),
            dma((sends,)), dma((slots,)),
            dma((nc - 1,)), dma((nc,)),
            dma((sends,)), dma((slots,)),
            dma((nc - 1,)), dma((nc,)),
            dma((nr - 1,)), dma((nr,)),
            dma((nc - 1,)), dma((nc,)),
        ],
        compiler_params=pltpu.CompilerParams(
            collective_id=0, has_side_effects=True, vmem_limit_bytes=48 * 1024 * 1024
        ),
        name="reflector_update",
    )(*(pltpu.with_memory_space_constraint(x, pltpu.HBM) for x in (reflectors.reshape(nc, h, n), matrix, factors[0])))


def solution(mesh):
    return jax.shard_map(
        shards,
        mesh=mesh,
        in_specs=(P("row", "col"), P(None, None, "row"), P()),
        out_specs=(P("row", "col"), P(None, None, "row")),
        check_vma=False,
    )
```

```python
import functools

import jax
import jax.numpy as jnp
from jax import lax
from jax.experimental import pallas as pl
from jax.experimental.pallas import tpu as pltpu
from jax.sharding import PartitionSpec as P

MESH = pl.DeviceIdType.MESH


def split(x):
    hi = x.astype(jnp.bfloat16)
    return hi, (x - hi.astype(jnp.float32)).astype(jnp.bfloat16)


def dot(a, b, da, db):
    return lax.dot_general(a, b, (((da,), (db,)), ((), ())), preferred_element_type=jnp.float32)


def dot3(a, b, da, db):
    ah, al = split(a)
    bh, bl = split(b)
    return dot(ah, bh, da, db) + (dot(ah, bl, da, db) + dot(al, bh, da, db))


def kernel(
    nr, nc, v_hbm, a_hbm, f_hbm, a_ref, left_ref, right_ref, w_ref,
    a_hi, a_lo, v_ref, f_ref, vrecv, pbuf, precv, yown, yrecv, yrow, srow, spart, sown, sfull,
    in_sem, gv_send, gv_recv, rs_send, rs_recv, gy_send, gy_recv, yr_send, yr_recv, sr_send, sr_recv, sc_send, sc_recv,
):
    ratio, half = nr // nc, nc // 2
    r, c = lax.axis_index("row"), lax.axis_index("col")
    g, i = r // ratio, r % ratio
    line, core = c // 2, c % 2
    aligned = g % 2 == core
    n = v_ref.shape[2]
    b = f_ref.shape[0]
    h = b // nc

    v_copy = pltpu.make_async_copy(v_hbm, v_ref, in_sem.at[0])
    a_copy = pltpu.make_async_copy(a_hbm, a_ref, in_sem.at[1])
    f_copy = pltpu.make_async_copy(f_hbm, f_ref, in_sem.at[2])
    v_copy.start()
    f_copy.start()
    a_copy.start()

    def remote(src, dst, send, recv, row, col):
        return pltpu.make_async_remote_copy(
            src_ref=src, dst_ref=dst, send_sem=send, recv_sem=recv, device_id=(row, col), device_id_type=MESH
        )

    row_peers = [lax.rem(r + k, nr) for k in range(1, nr)]
    col_peers = [lax.rem(c + k, nc) for k in range(1, nc)]

    def signal(row, col):
        pl.semaphore_signal(barrier, inc=1, device_id=(row, col), device_id_type=MESH)

    barrier = pltpu.get_barrier_semaphore()
    for t in row_peers:
        signal(t, c)
    for q in col_peers:
        signal(r, q)
    for d in range(ratio):
        for e in range(half):
            if d or e:
                signal(g * ratio + lax.rem(i + d, ratio), lax.rem(line + e, half) * 2 + core)
    for j in range(half):
        for e in range(2):
            row = (lax.rem(g // 2 + j, half) * 2 + core) * ratio + i
            col = line * 2 + lax.rem(core + e, 2)
            if j or e:
                signal(row, col)
            else:
                pl.when(jnp.logical_not(aligned))(functools.partial(signal, row, col))
    count = nr - 1 + nc - 1 + ratio * half - 1 + nc
    pl.semaphore_wait(barrier, count - jnp.where(aligned, 1, 0))

    relay = ratio * nc

    class Gather:
        def __init__(self, src, buf, send, recv):
            self.src, self.buf, self.send, self.recv = src, buf, send, recv
            self.slot = slot = jnp.where(g // 2 == line, i * nc + c, relay + (g // 2) * 2 + core)
            self.first = [
                remote(
                    src, buf.at[slot], send.at[j], recv.at[slot],
                    lax.rem(g + j, nc) * ratio + i, line * 2 + g % 2,
                )
                for j in range(nc)
            ]
            for copy in self.first[1:]:
                copy.start()
            pl.when(jnp.logical_not(aligned))(self.first[0].start)

        def forward(self, own):
            @pl.when(aligned)
            def _():
                self.buf[self.slot] = own[...]

            self.second = []
            k = nc
            for j in list(range(1, half)) + [0]:
                a = lax.rem(line + j, half)
                for e in range(2):
                    final = i * nc + line * 2 + e
                    slot = relay + a * 2 + e if j else final
                    mine = jnp.logical_and(a * 2 + core == g, e == core)
                    arrival = remote(self.src, self.buf.at[slot], self.send.at[0], self.recv.at[slot], r, c)
                    pl.when(jnp.logical_not(mine))(arrival.wait_recv)
                    for d in range(0 if j else 1, ratio):
                        copy = remote(
                            self.buf.at[slot], self.buf.at[final], self.send.at[k], self.recv.at[final],
                            g * ratio + lax.rem(i + d, ratio), a * 2 + core,
                        )
                        copy.start()
                        self.second.append(copy)
                        k += 1

        def wait(self):
            for d in range(ratio):
                for e in range(half):
                    for k in range(2):
                        if d or e:
                            slot = lax.rem(i + d, ratio) * nc + lax.rem(line + e, half) * 2 + k
                            remote(
                                self.src, self.buf.at[slot], self.send.at[0], self.recv.at[slot], r, c
                            ).wait_recv()

        def columns(self):
            return jnp.concatenate(
                [
                    jnp.concatenate([self.buf[t * nc + q] for q in range(nc)], axis=0)
                    for t in range(ratio)
                ],
                axis=1,
            )

        def end(self):
            pl.when(jnp.logical_not(aligned))(self.first[0].wait_send)
            for copy in self.first[1:] + self.second:
                copy.wait_send()

    gv = Gather(v_hbm.at[c], vrecv, gv_send, gv_recv)
    v_copy.wait()
    gv.forward(v_ref.at[c])

    f_copy.wait()
    a_copy.wait()
    hi, lo = split(a_ref[...])
    a_hi[...] = hi
    a_lo[...] = lo
    v_rows = jnp.concatenate([v_ref[q] for q in range(nc)], axis=0)

    gv.wait()
    v_cols = gv.columns()
    vh, vl = split(v_cols)
    both = dot(jnp.concatenate([vh, vl], axis=0), a_hi[...], 1, 1)
    partial = both[:b] + (both[b:] + dot(vh, a_lo[...], 1, 1))
    term = dot3(v_rows, partial, 1, 1)
    for q in range(nc):
        pbuf[q, :, :n] = partial[q * h:(q + 1) * h]
        pbuf[q, :, n:] = term[q * h:(q + 1) * h]

    rs = [remote(pbuf.at[q], precv.at[c], rs_send.at[k], rs_recv.at[c], r, q) for k, q in enumerate(col_peers)]
    for copy in rs:
        copy.start()
    total = pbuf[c]
    for k, q in enumerate(col_peers):
        remote(pbuf.at[q], precv.at[q], rs_send.at[k], rs_recv.at[q], r, q).wait_recv()
        total = total + precv[q]
    yown[...] = total[:, :n]
    spart[...] = total[:, n:]
    srow[r] = total[:, n:]

    sr = [remote(spart, srow.at[r], sr_send.at[k], sr_recv.at[r], t, c) for k, t in enumerate(row_peers)]
    for copy in sr:
        copy.start()
    gy = Gather(yown, yrecv, gy_send, gy_recv)
    yr = [remote(yown, yrow.at[c], yr_send.at[k], yr_recv.at[c], r, q) for k, q in enumerate(col_peers)]
    for copy in yr:
        copy.start()
    yrow[c] = yown[...]

    for k, t in enumerate(row_peers):
        remote(spart, srow.at[t], sr_send.at[k], sr_recv.at[t], t, c).wait_recv()
    s = srow[0]
    for t in range(1, nr):
        s = s + srow[t]
    sown[...] = s
    sfull[c] = s
    sc = [remote(sown, sfull.at[c], sc_send.at[k], sc_recv.at[c], r, q) for k, q in enumerate(col_peers)]
    for copy in sc:
        copy.start()
    gy.forward(yown)

    factor = f_ref[...]
    for k, q in enumerate(col_peers):
        remote(yown, yrow.at[q], yr_send.at[k], yr_recv.at[q], r, q).wait_recv()
    y_rows = jnp.concatenate([yrow[q] for q in range(nc)], axis=0)
    x_rows = dot3(factor, y_rows, 0, 0)
    for k, q in enumerate(col_peers):
        remote(sown, sfull.at[q], sc_send.at[k], sc_recv.at[q], r, q).wait_recv()
    square = jnp.concatenate([sfull[q] for q in range(nc)], axis=0)
    mixing = 0.5 * dot3(dot3(square, factor, 1, 0), factor, 0, 0)
    w_rows = x_rows - dot3(mixing, v_rows, 1, 0)
    w_ref[0] = w_rows
    lh, ll = split(jnp.concatenate([v_rows, w_rows], axis=0).T)
    left_ref[...] = jnp.concatenate([lh, lh, ll], axis=1)
    right_ref[b:2 * b] = vh
    right_ref[3 * b:4 * b] = vl
    right_ref[5 * b:] = vh
    mixed = dot3(mixing, v_cols, 1, 0)

    gy.wait()
    wh, wl = split(dot3(factor, gy.columns(), 0, 0) - mixed)
    right_ref[:b] = wh
    right_ref[2 * b:3 * b] = wl
    right_ref[4 * b:5 * b] = wh

    gv.end()
    gy.end()
    for copy in rs + sr + yr + sc:
        copy.wait_send()


def update(a_ref, left_ref, right_ref, w_ref, out_ref, companion_ref):
    size = out_ref.shape[0]
    rows = pl.ds(pl.multiple_of(pl.program_id(0) * size, size), size)
    out_ref[...] = a_ref[rows, :] - dot(left_ref[rows, :], right_ref[...], 1, 0)

    @pl.when(pl.program_id(0) == 0)
    def _():
        companion_ref[...] = w_ref[...]


def shards(matrix, reflectors, factors):
    nr, nc = lax.axis_size("row"), lax.axis_size("col")
    _, b, n = reflectors.shape
    m, k = matrix.shape
    ratio, h = nr // nc, b // nc
    f32 = jnp.float32
    dma = pltpu.SemaphoreType.DMA
    vmem = pl.BlockSpec(memory_space=pltpu.VMEM)
    hbm = pl.BlockSpec(memory_space=pltpu.HBM)
    slots = ratio * nc + nc
    sends = nc + 2 * (ratio * (nc // 2) - 1)
    held = pl.pallas_call(
        functools.partial(kernel, nr, nc),
        out_shape=(
            jax.ShapeDtypeStruct((m, k), f32),
            jax.ShapeDtypeStruct((m, 6 * b), jnp.bfloat16),
            jax.ShapeDtypeStruct((6 * b, k), jnp.bfloat16),
            jax.ShapeDtypeStruct((1, b, n), f32),
        ),
        in_specs=[hbm, hbm, hbm],
        out_specs=(vmem,) * 4,
        scratch_shapes=[
            pltpu.VMEM((m, k), jnp.bfloat16),
            pltpu.VMEM((m, k), jnp.bfloat16),
            pltpu.VMEM((nc, h, n), f32),
            pltpu.VMEM((b, b), f32),
            pltpu.VMEM((slots, h, n), f32),
            pltpu.VMEM((nc, h, n + b), f32),
            pltpu.VMEM((nc, h, n + b), f32),
            pltpu.VMEM((h, n), f32),
            pltpu.VMEM((slots, h, n), f32),
            pltpu.VMEM((nc, h, n), f32),
            pltpu.VMEM((nr, h, b), f32),
            pltpu.VMEM((h, b), f32),
            pltpu.VMEM((h, b), f32),
            pltpu.VMEM((nc, h, b), f32),
            dma((3,)),
            dma((sends,)), dma((slots,)),
            dma((nc - 1,)), dma((nc,)),
            dma((sends,)), dma((slots,)),
            dma((nc - 1,)), dma((nc,)),
            dma((nr - 1,)), dma((nr,)),
            dma((nc - 1,)), dma((nc,)),
        ],
        compiler_params=pltpu.CompilerParams(
            collective_id=0, has_side_effects=True, vmem_limit_bytes=32 * 1024 * 1024
        ),
        name="reflector_update",
    )(*(pltpu.with_memory_space_constraint(x, pltpu.HBM) for x in (reflectors.reshape(nc, h, n), matrix, factors[0])))
    steps = 4
    return pl.pallas_call(
        update,
        grid=(steps,),
        out_shape=(jax.ShapeDtypeStruct((m, k), f32), jax.ShapeDtypeStruct((1, b, n), f32)),
        in_specs=[vmem] * 4,
        out_specs=(
            pl.BlockSpec((m // steps, k), lambda t: (t, 0)),
            pl.BlockSpec((1, b, n), lambda t: (0, 0, 0)),
        ),
        compiler_params=pltpu.CompilerParams(vmem_limit_bytes=16 * 1024 * 1024),
        name="tile_update",
    )(*held)


def solution(mesh):
    return jax.shard_map(
        shards,
        mesh=mesh,
        in_specs=(P("row", "col"), P(None, None, "row"), P()),
        out_specs=(P("row", "col"), P(None, None, "row")),
        check_vma=False,
    )
```

```python
import functools

import jax
import jax.numpy as jnp
from jax import lax
from jax.experimental import pallas as pl
from jax.experimental.pallas import tpu as pltpu
from jax.sharding import PartitionSpec as P

MESH = pl.DeviceIdType.MESH


def split(x):
    hi = x.astype(jnp.bfloat16)
    return hi, (x - hi.astype(jnp.float32)).astype(jnp.bfloat16)


def dot(a, b, da, db):
    return lax.dot_general(a, b, (((da,), (db,)), ((), ())), preferred_element_type=jnp.float32)


def dot3(a, b, da, db):
    ah, al = split(a)
    bh, bl = split(b)
    return dot(ah, bh, da, db) + (dot(ah, bl, da, db) + dot(al, bh, da, db))


def kernel(
    nr, nc, v_hbm, a_hbm, f_hbm, a_ref, left_ref, right_ref, w_ref,
    v_ref, f_ref, vown, vrecv, zbuf, zrecv, ycols, yhalf, yrow, spart, scol, sfull,
    in_sem, gv_send, gv_recv, rs_send, rs_recv, ag_send, ag_recv, yr_send, yr_recv, sc_send, sc_recv, sr_send, sr_recv,
):
    ratio, half = nr // nc, nc // 2
    r, c = lax.axis_index("row"), lax.axis_index("col")
    g, i = r // ratio, r % ratio
    line, core = c // 2, c % 2
    aligned = g % 2 == core
    home = r // ratio
    n = v_hbm.shape[2]
    b = f_ref.shape[0]
    hr = b // nr

    v_copy = pltpu.make_async_copy(v_hbm, v_ref, in_sem.at[0])
    a_copy = pltpu.make_async_copy(a_hbm, a_ref, in_sem.at[1])
    f_copy = pltpu.make_async_copy(f_hbm, f_ref, in_sem.at[2])
    v_copy.start()
    f_copy.start()
    a_copy.start()

    def remote(src, dst, send, recv, row, col):
        return pltpu.make_async_remote_copy(
            src_ref=src, dst_ref=dst, send_sem=send, recv_sem=recv, device_id=(row, col), device_id_type=MESH
        )

    row_peers = [lax.rem(r + k, nr) for k in range(1, nr)]
    col_peers = [lax.rem(c + k, nc) for k in range(1, nc)]

    def signal(row, col):
        pl.semaphore_signal(barrier, inc=1, device_id=(row, col), device_id_type=MESH)

    barrier = pltpu.get_barrier_semaphore()
    for t in row_peers:
        signal(t, c)
    for q in col_peers:
        signal(r, q)
    for d in range(1, ratio):
        for e in range(1, half):
            signal(g * ratio + lax.rem(i + d, ratio), lax.rem(line + e, half) * 2 + core)
    for a in range(half):
        signal((a * 2 + core) * ratio + i, line * 2 + 1 - core)

    @pl.when(home != c)
    def _():
        for t in range(nr):
            signal(t, home)

    count = nr - 1 + nc - 1 + (ratio - 1) * (half - 1) + ratio * (nc - 1)
    pl.semaphore_wait(barrier, count + jnp.where(aligned, 0, nc))

    relay = ratio * nc

    class Gather:
        def __init__(self, src, buf, send, recv):
            self.src, self.buf, self.send, self.recv = src, buf, send, recv
            self.slot = slot = jnp.where(g // 2 == line, i * nc + c, relay + (g // 2) * 2 + core)
            self.first = [
                remote(
                    src, buf.at[slot], send.at[j], recv.at[slot],
                    lax.rem(g + j, nc) * ratio + i, line * 2 + g % 2,
                )
                for j in range(nc)
            ]
            for copy in self.first[1:]:
                copy.start()
            pl.when(jnp.logical_not(aligned))(self.first[0].start)

        def forward(self, own):
            @pl.when(aligned)
            def _():
                self.buf[self.slot] = own[...]

            self.second = []
            k = nc
            for j in list(range(1, half)) + [0]:
                a = lax.rem(line + j, half)
                for e in range(2):
                    final = i * nc + line * 2 + e
                    slot = relay + a * 2 + e if j else final
                    mine = jnp.logical_and(a * 2 + core == g, e == core)
                    arrival = remote(self.src, self.buf.at[slot], self.send.at[0], self.recv.at[slot], r, c)
                    pl.when(jnp.logical_not(mine))(arrival.wait_recv)
                    for d in range(0 if j else 1, ratio):
                        copy = remote(
                            self.buf.at[slot], self.buf.at[final], self.send.at[k], self.recv.at[final],
                            g * ratio + lax.rem(i + d, ratio), a * 2 + core,
                        )
                        copy.start()
                        self.second.append(copy)
                        k += 1

        def wait(self):
            for d in range(ratio):
                for e in range(half):
                    for k in range(2):
                        if d or e:
                            slot = lax.rem(i + d, ratio) * nc + lax.rem(line + e, half) * 2 + k
                            remote(
                                self.src, self.buf.at[slot], self.send.at[0], self.recv.at[slot], r, c
                            ).wait_recv()

        def columns(self):
            return jnp.concatenate(
                [
                    jnp.concatenate([self.buf[t * nc + q, :, :n] for q in range(nc)], axis=0)
                    for t in range(ratio)
                ],
                axis=1,
            )

        def end(self):
            pl.when(jnp.logical_not(aligned))(self.first[0].wait_send)
            for copy in self.first[1:] + self.second:
                copy.wait_send()

    v_copy.wait()
    vown[:, :n] = v_ref[c]
    gv = Gather(vown, vrecv, gv_send, gv_recv)
    v_rows = jnp.concatenate([v_ref[q] for q in range(nc)], axis=0)
    vh, vl = split(v_rows)
    f_copy.wait()
    a_copy.wait()
    ah, al = split(a_ref[...])
    both = dot(jnp.concatenate([vh, vl], axis=0), ah, 1, 0)
    z = both[:b] + (both[b:] + dot(vh, al, 1, 0))
    for t in range(nr):
        zbuf[t] = z[t * hr:(t + 1) * hr]

    rs = [remote(zbuf.at[t], zrecv.at[r], rs_send.at[k], rs_recv.at[r], t, c) for k, t in enumerate(row_peers)]
    for copy in rs:
        copy.start()
    zrecv[r] = zbuf[r]

    gv.forward(vown)
    left_ref[:, :b] = vh.T
    left_ref[:, 2 * b:3 * b] = vh.T
    left_ref[:, 4 * b:5 * b] = vl.T
    gv.wait()
    v_cols = gv.columns()
    ch, cl = split(v_cols)
    right_ref[b:2 * b] = ch
    right_ref[3 * b:4 * b] = cl
    right_ref[5 * b:] = ch

    for k, t in enumerate(row_peers):
        remote(zbuf.at[t], zrecv.at[t], rs_send.at[k], rs_recv.at[t], t, c).wait_recv()
    y = zrecv[0]
    for t in range(1, nr):
        y = y + zrecv[t]
    ycols[r] = y
    for e in range(ratio):
        yhalf[e, :, :n] = y[:, e * n:(e + 1) * n]
    ag = [remote(ycols.at[r], ycols.at[r], ag_send.at[k], ag_recv.at[r], t, c) for k, t in enumerate(row_peers)]
    for copy in ag:
        copy.start()

    scol[c, :, :b] = dot3(y, v_cols, 1, 1)
    sc = [remote(scol.at[c], scol.at[c], sc_send.at[k], sc_recv.at[c], r, q) for k, q in enumerate(col_peers)]
    for copy in sc:
        copy.start()

    yr = []
    for d in range(nc):
        q = lax.rem(c + d, nc)
        for e in range(ratio):
            t = c * ratio + e
            copy = remote(yhalf.at[e], yrow.at[r], yr_send.at[d, e], yr_recv.at[r], t, q)
            yr.append((d or None, t, copy))
            if d:
                copy.start()
            else:
                pl.when(t != r)(copy.start)

    @pl.when(home == c)
    def _():
        yrow[r] = yhalf[i]

    for k, q in enumerate(col_peers):
        remote(scol.at[c], scol.at[q], sc_send.at[k], sc_recv.at[q], r, q).wait_recv()
    s = scol[0]
    for q in range(1, nc):
        s = s + scol[q]
    spart[...] = s
    sfull[r] = s
    sr = [remote(spart, sfull.at[r], sr_send.at[k], sr_recv.at[r], t, c) for k, t in enumerate(row_peers)]
    for copy in sr:
        copy.start()

    factor = f_ref[...]
    for d in range(nr):
        t = lax.rem(r + d, nr)
        arrival = remote(yhalf.at[0], yrow.at[t], yr_send.at[0, 0], yr_recv.at[t], t, home)
        if d:
            arrival.wait_recv()
        else:
            pl.when(home != c)(arrival.wait_recv)
    x_rows = dot3(factor, jnp.concatenate([yrow[t, :, :n] for t in range(nr)], axis=0), 0, 0)
    for k, t in enumerate(row_peers):
        remote(ycols.at[r], ycols.at[t], ag_send.at[k], ag_recv.at[t], t, c).wait_recv()
    x_cols = dot3(factor, jnp.concatenate([ycols[t] for t in range(nr)], axis=0), 0, 0)
    for k, t in enumerate(row_peers):
        remote(spart, sfull.at[t], sr_send.at[k], sr_recv.at[t], t, c).wait_recv()
    square = jnp.concatenate([sfull[t, :, :b] for t in range(nr)], axis=0)
    mixing = 0.5 * dot3(factor, dot3(square, factor, 1, 0), 0, 0)
    w_rows = x_rows - dot3(mixing, v_rows, 1, 0)
    w_ref[0] = w_rows
    lh, ll = split(w_rows.T)
    left_ref[:, b:2 * b] = lh
    left_ref[:, 3 * b:4 * b] = lh
    left_ref[:, 5 * b:] = ll
    wh, wl = split(x_cols - dot3(mixing, v_cols, 1, 0))
    right_ref[:b] = wh
    right_ref[2 * b:3 * b] = wl
    right_ref[4 * b:5 * b] = wh

    gv.end()
    for copy in rs + ag + sc + sr:
        copy.wait_send()
    for d, t, copy in yr:
        if d:
            copy.wait_send()
        else:
            pl.when(t != r)(copy.wait_send)


def update(a_ref, left_ref, right_ref, w_ref, out_ref, companion_ref):
    size = out_ref.shape[0]
    rows = pl.ds(pl.multiple_of(pl.program_id(0) * size, size), size)
    out_ref[...] = a_ref[rows, :] - dot(left_ref[rows, :], right_ref[...], 1, 0)

    @pl.when(pl.program_id(0) == 0)
    def _():
        companion_ref[...] = w_ref[...]


def shards(matrix, reflectors, factors):
    nr, nc = lax.axis_size("row"), lax.axis_size("col")
    _, b, n = reflectors.shape
    m, k = matrix.shape
    ratio, h, hr = nr // nc, b // nc, b // nr
    wide = pl.cdiv(n, 128) * 128
    f32 = jnp.float32
    dma = pltpu.SemaphoreType.DMA
    vmem = pl.BlockSpec(memory_space=pltpu.VMEM)
    hbm = pl.BlockSpec(memory_space=pltpu.HBM)
    slots = ratio * nc + nc
    sends = nc + 2 * (ratio * (nc // 2) - 1)
    held = pl.pallas_call(
        functools.partial(kernel, nr, nc),
        out_shape=(
            jax.ShapeDtypeStruct((m, k), f32),
            jax.ShapeDtypeStruct((m, 6 * b), jnp.bfloat16),
            jax.ShapeDtypeStruct((6 * b, k), jnp.bfloat16),
            jax.ShapeDtypeStruct((1, b, n), f32),
        ),
        in_specs=[hbm, hbm, hbm],
        out_specs=(vmem,) * 4,
        scratch_shapes=[
            pltpu.VMEM((nc, h, n), f32),
            pltpu.VMEM((b, b), f32),
            pltpu.VMEM((h, wide), f32),
            pltpu.VMEM((slots, h, wide), f32),
            pltpu.VMEM((nr, hr, k), f32),
            pltpu.VMEM((nr, hr, k), f32),
            pltpu.VMEM((nr, hr, k), f32),
            pltpu.VMEM((ratio, hr, wide), f32),
            pltpu.VMEM((nr, hr, wide), f32),
            pltpu.VMEM((hr, 128), f32),
            pltpu.VMEM((nc, hr, 128), f32),
            pltpu.VMEM((nr, hr, 128), f32),
            dma((3,)),
            dma((sends,)), dma((slots,)),
            dma((nr - 1,)), dma((nr,)),
            dma((nr - 1,)), dma((nr,)),
            dma((nc, ratio)), dma((nr,)),
            dma((nc - 1,)), dma((nc,)),
            dma((nr - 1,)), dma((nr,)),
        ],
        compiler_params=pltpu.CompilerParams(
            collective_id=0, has_side_effects=True, vmem_limit_bytes=32 * 1024 * 1024
        ),
        name="reflector_update",
    )(*(pltpu.with_memory_space_constraint(x, pltpu.HBM) for x in (reflectors.reshape(nc, h, n), matrix, factors[0])))
    steps = 4
    return pl.pallas_call(
        update,
        grid=(steps,),
        out_shape=(jax.ShapeDtypeStruct((m, k), f32), jax.ShapeDtypeStruct((1, b, n), f32)),
        in_specs=[vmem] * 4,
        out_specs=(
            pl.BlockSpec((m // steps, k), lambda t: (t, 0)),
            pl.BlockSpec((1, b, n), lambda t: (0, 0, 0)),
        ),
        compiler_params=pltpu.CompilerParams(vmem_limit_bytes=16 * 1024 * 1024),
        name="tile_update",
    )(*held)


def solution(mesh):
    return jax.shard_map(
        shards,
        mesh=mesh,
        in_specs=(P("row", "col"), P(None, None, "row"), P()),
        out_specs=(P("row", "col"), P(None, None, "row")),
        check_vma=False,
    )
```

```python
import functools

import jax
import jax.numpy as jnp
from jax import lax
from jax.experimental import pallas as pl
from jax.experimental.pallas import tpu as pltpu
from jax.sharding import PartitionSpec as P

MESH = pl.DeviceIdType.MESH


def split(x):
    hi = x.astype(jnp.bfloat16)
    return hi, (x - hi.astype(jnp.float32)).astype(jnp.bfloat16)


def dot(a, b, da, db):
    return lax.dot_general(a, b, (((da,), (db,)), ((), ())), preferred_element_type=jnp.float32)


def dot3(a, b, da, db):
    ah, al = split(a)
    bh, bl = split(b)
    return dot(ah, bh, da, db) + (dot(ah, bl, da, db) + dot(al, bh, da, db))


def wrap(x, size):
    return jnp.where(x >= size, x - size, x)


def kernel(
    nr, nc, v_hbm, a_hbm, f_hbm, a_ref, left_ref, right_ref, w_ref,
    a_hi, a_lo, v_ref, f_ref, vown, vrecv, pbuf, precv, yown, yrecv, yrow, srow, spart, sown, sfull,
    in_sem, gv_send, gv_recv, rs_send, rs_recv, gy_send, gy_recv, yr_send, yr_recv, sr_send, sr_recv, sc_send, sc_recv,
):
    ratio, half = nr // nc, nc // 2
    r, c = lax.axis_index("row"), lax.axis_index("col")
    g, i = r // ratio, r % ratio
    line, core = c // 2, c % 2
    aligned = g % 2 == core
    n = v_hbm.shape[2]
    b = f_ref.shape[0]
    h = b // nc

    v_copy = pltpu.make_async_copy(v_hbm, v_ref, in_sem.at[0])
    a_copy = pltpu.make_async_copy(a_hbm, a_ref, in_sem.at[1])
    f_copy = pltpu.make_async_copy(f_hbm, f_ref, in_sem.at[2])
    v_copy.start()
    f_copy.start()
    a_copy.start()

    def remote(src, dst, send, recv, row, col):
        return pltpu.make_async_remote_copy(
            src_ref=src, dst_ref=dst, send_sem=send, recv_sem=recv, device_id=(row, col), device_id_type=MESH
        )

    row_peers = [wrap(r + k, nr) for k in range(1, nr)]
    col_peers = [wrap(c + k, nc) for k in range(1, nc)]

    def signal(row, col):
        pl.semaphore_signal(barrier, inc=1, device_id=(row, col), device_id_type=MESH)

    barrier = pltpu.get_barrier_semaphore()
    for t in row_peers:
        signal(t, c)
    for q in col_peers:
        signal(r, q)
    for d in range(ratio):
        for e in range(half):
            if d or e:
                signal(g * ratio + wrap(i + d, ratio), wrap(line + e, half) * 2 + core)
    for j in range(half):
        for e in range(2):
            row = (wrap(g // 2 + j, half) * 2 + core) * ratio + i
            col = line * 2 + wrap(core + e, 2)
            if j or e:
                signal(row, col)
            else:
                pl.when(jnp.logical_not(aligned))(functools.partial(signal, row, col))
    count = nr - 1 + nc - 1 + ratio * half - 1 + nc
    pl.semaphore_wait(barrier, count - jnp.where(aligned, 1, 0))

    relay = ratio * nc

    class Gather:
        def __init__(self, src, buf, send, recv):
            self.src, self.buf, self.send, self.recv = src, buf, send, recv
            self.slot = slot = jnp.where(g // 2 == line, i * nc + c, relay + (g // 2) * 2 + core)
            self.first = [
                remote(
                    src, buf.at[slot], send.at[j], recv.at[slot],
                    wrap(g + j, nc) * ratio + i, line * 2 + g % 2,
                )
                for j in range(nc)
            ]
            for copy in self.first[1:]:
                copy.start()
            pl.when(jnp.logical_not(aligned))(self.first[0].start)

        def forward(self, own):
            @pl.when(aligned)
            def _():
                self.buf[self.slot] = own[...]

            self.second = []
            k = nc
            for j in list(range(1, half)) + [0]:
                a = wrap(line + j, half)
                for e in range(2):
                    final = i * nc + line * 2 + e
                    slot = relay + a * 2 + e if j else final
                    mine = jnp.logical_and(a * 2 + core == g, e == core)
                    arrival = remote(self.src, self.buf.at[slot], self.send.at[0], self.recv.at[slot], r, c)
                    pl.when(jnp.logical_not(mine))(arrival.wait_recv)
                    for d in range(0 if j else 1, ratio):
                        copy = remote(
                            self.buf.at[slot], self.buf.at[final], self.send.at[k], self.recv.at[final],
                            g * ratio + wrap(i + d, ratio), a * 2 + core,
                        )
                        copy.start()
                        self.second.append(copy)
                        k += 1

        def wait(self):
            for d in range(ratio):
                for e in range(half):
                    for k in range(2):
                        if d or e:
                            slot = wrap(i + d, ratio) * nc + wrap(line + e, half) * 2 + k
                            remote(
                                self.src, self.buf.at[slot], self.send.at[0], self.recv.at[slot], r, c
                            ).wait_recv()

        def columns(self):
            return jnp.concatenate(
                [
                    jnp.concatenate([self.buf[t * nc + q, :, :n] for q in range(nc)], axis=0)
                    for t in range(ratio)
                ],
                axis=1,
            )

        def end(self):
            pl.when(jnp.logical_not(aligned))(self.first[0].wait_send)
            for copy in self.first[1:] + self.second:
                copy.wait_send()

    v_copy.wait()
    vown[:, :n] = v_ref[c]
    gv = Gather(vown, vrecv, gv_send, gv_recv)
    gv.forward(vown)

    f_copy.wait()
    a_copy.wait()
    hi, lo = split(a_ref[...])
    a_hi[...] = hi
    a_lo[...] = lo
    v_rows = jnp.concatenate([v_ref[q] for q in range(nc)], axis=0)

    gv.wait()
    v_cols = gv.columns()
    vh, vl = split(v_cols)
    both = dot(jnp.concatenate([vh, vl], axis=0), a_hi[...], 1, 1)
    partial = both[:b] + (both[b:] + dot(vh, a_lo[...], 1, 1))
    term = dot3(v_rows, partial, 1, 1)
    for q in range(nc):
        pbuf[q, :, :n] = partial[q * h:(q + 1) * h]
        pbuf[q, :, n:] = term[q * h:(q + 1) * h]

    rs = [remote(pbuf.at[q], precv.at[c], rs_send.at[k], rs_recv.at[c], r, q) for k, q in enumerate(col_peers)]
    for copy in rs:
        copy.start()
    total = pbuf[c]
    for k, q in enumerate(col_peers):
        remote(pbuf.at[q], precv.at[q], rs_send.at[k], rs_recv.at[q], r, q).wait_recv()
        total = total + precv[q]
    yown[...] = total
    spart[:, :b] = total[:, n:]
    srow[r, :, :b] = total[:, n:]

    sr = [remote(spart, srow.at[r], sr_send.at[k], sr_recv.at[r], t, c) for k, t in enumerate(row_peers)]
    for copy in sr:
        copy.start()
    gy = Gather(yown, yrecv, gy_send, gy_recv)
    yr = [remote(yown, yrow.at[c], yr_send.at[k], yr_recv.at[c], r, q) for k, q in enumerate(col_peers)]
    for copy in yr:
        copy.start()
    yrow[c] = yown[...]

    for k, t in enumerate(row_peers):
        remote(spart, srow.at[t], sr_send.at[k], sr_recv.at[t], t, c).wait_recv()
    s = srow[0]
    for t in range(1, nr):
        s = s + srow[t]
    sown[...] = s
    sfull[c] = s
    sc = [remote(sown, sfull.at[c], sc_send.at[k], sc_recv.at[c], r, q) for k, q in enumerate(col_peers)]
    for copy in sc:
        copy.start()
    gy.forward(yown)

    factor = f_ref[...]
    for k, q in enumerate(col_peers):
        remote(yown, yrow.at[q], yr_send.at[k], yr_recv.at[q], r, q).wait_recv()
    y_rows = jnp.concatenate([yrow[q, :, :n] for q in range(nc)], axis=0)
    x_rows = dot3(factor, y_rows, 0, 0)
    for k, q in enumerate(col_peers):
        remote(sown, sfull.at[q], sc_send.at[k], sc_recv.at[q], r, q).wait_recv()
    square = jnp.concatenate([sfull[q, :, :b] for q in range(nc)], axis=0)
    mixing = 0.5 * dot3(dot3(square, factor, 1, 0), factor, 0, 0)
    w_rows = x_rows - dot3(mixing, v_rows, 1, 0)
    w_ref[0] = w_rows
    lh, ll = split(jnp.concatenate([v_rows, w_rows], axis=0).T)
    left_ref[...] = jnp.concatenate([lh, lh, ll], axis=1)
    right_ref[b:2 * b] = vh
    right_ref[3 * b:4 * b] = vl
    right_ref[5 * b:] = vh
    mixed = dot3(mixing, v_cols, 1, 0)

    gy.wait()
    wh, wl = split(dot3(factor, gy.columns(), 0, 0) - mixed)
    right_ref[:b] = wh
    right_ref[2 * b:3 * b] = wl
    right_ref[4 * b:5 * b] = wh

    gv.end()
    gy.end()
    for copy in rs + sr + yr + sc:
        copy.wait_send()


def update(a_ref, left_ref, right_ref, w_ref, out_ref, companion_ref):
    size = out_ref.shape[0]
    rows = pl.ds(pl.multiple_of(pl.program_id(0) * size, size), size)
    out_ref[...] = a_ref[rows, :] - dot(left_ref[rows, :], right_ref[...], 1, 0)

    @pl.when(pl.program_id(0) == 0)
    def _():
        companion_ref[...] = w_ref[...]


def shards(matrix, reflectors, factors):
    nr, nc = lax.axis_size("row"), lax.axis_size("col")
    _, b, n = reflectors.shape
    m, k = matrix.shape
    ratio, h = nr // nc, b // nc
    f32 = jnp.float32
    dma = pltpu.SemaphoreType.DMA
    vmem = pl.BlockSpec(memory_space=pltpu.VMEM)
    hbm = pl.BlockSpec(memory_space=pltpu.HBM)
    slots = ratio * nc + nc
    sends = nc + 2 * (ratio * (nc // 2) - 1)
    held = pl.pallas_call(
        functools.partial(kernel, nr, nc),
        out_shape=(
            jax.ShapeDtypeStruct((m, k), f32),
            jax.ShapeDtypeStruct((m, 6 * b), jnp.bfloat16),
            jax.ShapeDtypeStruct((6 * b, k), jnp.bfloat16),
            jax.ShapeDtypeStruct((1, b, n), f32),
        ),
        in_specs=[hbm, hbm, hbm],
        out_specs=(vmem,) * 4,
        scratch_shapes=[
            pltpu.VMEM((m, k), jnp.bfloat16),
            pltpu.VMEM((m, k), jnp.bfloat16),
            pltpu.VMEM((nc, h, n), f32),
            pltpu.VMEM((b, b), f32),
            pltpu.VMEM((h, n + b), f32),
            pltpu.VMEM((slots, h, n + b), f32),
            pltpu.VMEM((nc, h, n + b), f32),
            pltpu.VMEM((nc, h, n + b), f32),
            pltpu.VMEM((h, n + b), f32),
            pltpu.VMEM((slots, h, n + b), f32),
            pltpu.VMEM((nc, h, n + b), f32),
            pltpu.VMEM((nr, h, 2 * b), f32),
            pltpu.VMEM((h, 2 * b), f32),
            pltpu.VMEM((h, 2 * b), f32),
            pltpu.VMEM((nc, h, 2 * b), f32),
            dma((3,)),
            dma((sends,)), dma((slots,)),
            dma((nc - 1,)), dma((nc,)),
            dma((sends,)), dma((slots,)),
            dma((nc - 1,)), dma((nc,)),
            dma((nr - 1,)), dma((nr,)),
            dma((nc - 1,)), dma((nc,)),
        ],
        compiler_params=pltpu.CompilerParams(
            collective_id=0, has_side_effects=True, vmem_limit_bytes=32 * 1024 * 1024
        ),
        name="reflector_update",
    )(*(pltpu.with_memory_space_constraint(x, pltpu.HBM) for x in (reflectors.reshape(nc, h, n), matrix, factors[0])))
    steps = 2
    return pl.pallas_call(
        update,
        grid=(steps,),
        out_shape=(jax.ShapeDtypeStruct((m, k), f32), jax.ShapeDtypeStruct((1, b, n), f32)),
        in_specs=[vmem] * 4,
        out_specs=(
            pl.BlockSpec((m // steps, k), lambda t: (t, 0)),
            pl.BlockSpec((1, b, n), lambda t: (0, 0, 0)),
        ),
        compiler_params=pltpu.CompilerParams(vmem_limit_bytes=16 * 1024 * 1024),
        name="tile_update",
    )(*held)


def solution(mesh):
    return jax.shard_map(
        shards,
        mesh=mesh,
        in_specs=(P("row", "col"), P(None, None, "row"), P()),
        out_specs=(P("row", "col"), P(None, None, "row")),
        check_vma=False,
    )
```

```python
import functools

import jax
import jax.numpy as jnp
from jax import lax
from jax.experimental import pallas as pl
from jax.experimental.pallas import tpu as pltpu
from jax.sharding import PartitionSpec as P

MESH = pl.DeviceIdType.MESH


def split(x):
    hi = x.astype(jnp.bfloat16)
    return hi, (x - hi.astype(jnp.float32)).astype(jnp.bfloat16)


def dot(a, b, da, db):
    return lax.dot_general(a, b, (((da,), (db,)), ((), ())), preferred_element_type=jnp.float32)


def dot3(a, b, da, db):
    ah, al = split(a)
    bh, bl = split(b)
    return dot(ah, bh, da, db) + (dot(ah, bl, da, db) + dot(al, bh, da, db))


def wrap(x, size):
    return jnp.where(x >= size, x - size, x)


def kernel(
    nr, nc, v_hbm, a_hbm, f_hbm, a_ref, left_ref, right_ref, w_ref,
    a_hi, a_lo, v_ref, f_ref, vown, vrecv, pbuf, precv, yown, yrecv, yrow, srow, spart, sown, sfull,
    in_sem, gv_send, gv_recv, rs_send, rs_recv, gy_send, gy_recv, yr_send, yr_recv, sr_send, sr_recv, sc_send, sc_recv,
):
    ratio = nr // nc
    r, c = lax.axis_index("row"), lax.axis_index("col")
    home, i = r // ratio, r % ratio
    at_home = home == c
    n = v_hbm.shape[2]
    b = f_ref.shape[0]
    h = b // nc

    v_copy = pltpu.make_async_copy(v_hbm, v_ref, in_sem.at[0])
    a_copy = pltpu.make_async_copy(a_hbm, a_ref, in_sem.at[1])
    f_copy = pltpu.make_async_copy(f_hbm, f_ref, in_sem.at[2])
    v_copy.start()
    f_copy.start()
    a_copy.start()

    def remote(src, dst, send, recv, row, col):
        return pltpu.make_async_remote_copy(
            src_ref=src, dst_ref=dst, send_sem=send, recv_sem=recv, device_id=(row, col), device_id_type=MESH
        )

    row_peers = [wrap(r + k, nr) for k in range(1, nr)]
    col_peers = [wrap(c + k, nc) for k in range(1, nc)]

    def signal(row, col):
        pl.semaphore_signal(barrier, inc=1, device_id=(row, col), device_id_type=MESH)

    barrier = pltpu.get_barrier_semaphore()
    for t in row_peers:
        signal(t, c)
    for q in col_peers:
        signal(r, q)
    for q in col_peers:
        for e in range(ratio):
            signal(c * ratio + e, q)
    pl.semaphore_wait(barrier, nr - 1 + nc - 1 + jnp.where(at_home, 0, nr))

    class Gather:
        def __init__(self, src, buf, send, recv):
            self.src, self.buf, self.send, self.recv = src, buf, send, recv
            self.copies = [
                remote(src, buf.at[i, c], send.at[k], recv.at[i, c], wrap(r + k, nr), home) for k in range(nr)
            ]
            for copy in self.copies[1:]:
                copy.start()
            pl.when(jnp.logical_not(at_home))(self.copies[0].start)

            @pl.when(at_home)
            def _():
                buf[i, c] = src[...]

        def wait(self):
            for j in range(nc):
                q = wrap(c + j, nc)
                for e in range(ratio):
                    arrival = remote(self.src, self.buf.at[e, q], self.send.at[0], self.recv.at[e, q], r, c)
                    if j:
                        arrival.wait_recv()
                    else:
                        pl.when(c * ratio + e != r)(arrival.wait_recv)

        def columns(self):
            return jnp.concatenate(
                [jnp.concatenate([self.buf[t, q, :, :n] for q in range(nc)], axis=0) for t in range(ratio)],
                axis=1,
            )

        def end(self):
            pl.when(jnp.logical_not(at_home))(self.copies[0].wait_send)
            for copy in self.copies[1:]:
                copy.wait_send()

    v_copy.wait()
    vown[:, :n] = v_ref[c]
    gv = Gather(vown, vrecv, gv_send, gv_recv)

    f_copy.wait()
    a_copy.wait()
    hi, lo = split(a_ref[...])
    a_hi[...] = hi
    a_lo[...] = lo
    v_rows = jnp.concatenate([v_ref[q] for q in range(nc)], axis=0)

    gv.wait()
    v_cols = gv.columns()
    vh, vl = split(v_cols)
    both = dot(jnp.concatenate([vh, vl], axis=0), a_hi[...], 1, 1)
    partial = both[:b] + (both[b:] + dot(vh, a_lo[...], 1, 1))
    term = dot3(v_rows, partial, 1, 1)
    for q in range(nc):
        pbuf[q, :, :n] = partial[q * h:(q + 1) * h]
        pbuf[q, :, n:] = term[q * h:(q + 1) * h]

    rs = [remote(pbuf.at[q], precv.at[c], rs_send.at[k], rs_recv.at[c], r, q) for k, q in enumerate(col_peers)]
    for copy in rs:
        copy.start()
    total = pbuf[c]
    for k, q in enumerate(col_peers):
        remote(pbuf.at[q], precv.at[q], rs_send.at[k], rs_recv.at[q], r, q).wait_recv()
        total = total + precv[q]
    yown[...] = total
    spart[:, :b] = total[:, n:]
    srow[r, :, :b] = total[:, n:]

    sr = [remote(spart, srow.at[r], sr_send.at[k], sr_recv.at[r], t, c) for k, t in enumerate(row_peers)]
    for copy in sr:
        copy.start()
    gy = Gather(yown, yrecv, gy_send, gy_recv)
    yr = [remote(yown, yrow.at[c], yr_send.at[k], yr_recv.at[c], r, q) for k, q in enumerate(col_peers)]
    for copy in yr:
        copy.start()
    yrow[c] = yown[...]

    for k, t in enumerate(row_peers):
        remote(spart, srow.at[t], sr_send.at[k], sr_recv.at[t], t, c).wait_recv()
    s = srow[0]
    for t in range(1, nr):
        s = s + srow[t]
    sown[...] = s
    sfull[c] = s
    sc = [remote(sown, sfull.at[c], sc_send.at[k], sc_recv.at[c], r, q) for k, q in enumerate(col_peers)]
    for copy in sc:
        copy.start()

    factor = f_ref[...]
    for k, q in enumerate(col_peers):
        remote(yown, yrow.at[q], yr_send.at[k], yr_recv.at[q], r, q).wait_recv()
    y_rows = jnp.concatenate([yrow[q, :, :n] for q in range(nc)], axis=0)
    x_rows = dot3(factor, y_rows, 0, 0)
    for k, q in enumerate(col_peers):
        remote(sown, sfull.at[q], sc_send.at[k], sc_recv.at[q], r, q).wait_recv()
    square = jnp.concatenate([sfull[q, :, :b] for q in range(nc)], axis=0)
    mixing = 0.5 * dot3(dot3(square, factor, 1, 0), factor, 0, 0)
    w_rows = x_rows - dot3(mixing, v_rows, 1, 0)
    w_ref[0] = w_rows
    lh, ll = split(jnp.concatenate([v_rows, w_rows], axis=0).T)
    left_ref[...] = jnp.concatenate([lh, lh, ll], axis=1)
    right_ref[b:2 * b] = vh
    right_ref[3 * b:4 * b] = vl
    right_ref[5 * b:] = vh
    mixed = dot3(mixing, v_cols, 1, 0)

    gy.wait()
    wh, wl = split(dot3(factor, gy.columns(), 0, 0) - mixed)
    right_ref[:b] = wh
    right_ref[2 * b:3 * b] = wl
    right_ref[4 * b:5 * b] = wh

    gv.end()
    gy.end()
    for copy in rs + sr + yr + sc:
        copy.wait_send()


def update(a_ref, left_ref, right_ref, w_ref, out_ref, companion_ref):
    size = out_ref.shape[0]
    rows = pl.ds(pl.multiple_of(pl.program_id(0) * size, size), size)
    out_ref[...] = a_ref[rows, :] - dot(left_ref[rows, :], right_ref[...], 1, 0)

    @pl.when(pl.program_id(0) == 0)
    def _():
        companion_ref[...] = w_ref[...]


def shards(matrix, reflectors, factors):
    nr, nc = lax.axis_size("row"), lax.axis_size("col")
    _, b, n = reflectors.shape
    m, k = matrix.shape
    ratio, h = nr // nc, b // nc
    f32 = jnp.float32
    dma = pltpu.SemaphoreType.DMA
    vmem = pl.BlockSpec(memory_space=pltpu.VMEM)
    hbm = pl.BlockSpec(memory_space=pltpu.HBM)
    held = pl.pallas_call(
        functools.partial(kernel, nr, nc),
        out_shape=(
            jax.ShapeDtypeStruct((m, k), f32),
            jax.ShapeDtypeStruct((m, 6 * b), jnp.bfloat16),
            jax.ShapeDtypeStruct((6 * b, k), jnp.bfloat16),
            jax.ShapeDtypeStruct((1, b, n), f32),
        ),
        in_specs=[hbm, hbm, hbm],
        out_specs=(vmem,) * 4,
        scratch_shapes=[
            pltpu.VMEM((m, k), jnp.bfloat16),
            pltpu.VMEM((m, k), jnp.bfloat16),
            pltpu.VMEM((nc, h, n), f32),
            pltpu.VMEM((b, b), f32),
            pltpu.VMEM((h, n + b), f32),
            pltpu.VMEM((ratio, nc, h, n + b), f32),
            pltpu.VMEM((nc, h, n + b), f32),
            pltpu.VMEM((nc, h, n + b), f32),
            pltpu.VMEM((h, n + b), f32),
            pltpu.VMEM((ratio, nc, h, n + b), f32),
            pltpu.VMEM((nc, h, n + b), f32),
            pltpu.VMEM((nr, h, 2 * b), f32),
            pltpu.VMEM((h, 2 * b), f32),
            pltpu.VMEM((h, 2 * b), f32),
            pltpu.VMEM((nc, h, 2 * b), f32),
            dma((3,)),
            dma((nr,)), dma((ratio, nc)),
            dma((nc - 1,)), dma((nc,)),
            dma((nr,)), dma((ratio, nc)),
            dma((nc - 1,)), dma((nc,)),
            dma((nr - 1,)), dma((nr,)),
            dma((nc - 1,)), dma((nc,)),
        ],
        compiler_params=pltpu.CompilerParams(
            collective_id=0, has_side_effects=True, vmem_limit_bytes=32 * 1024 * 1024
        ),
        name="reflector_update",
    )(*(pltpu.with_memory_space_constraint(x, pltpu.HBM) for x in (reflectors.reshape(nc, h, n), matrix, factors[0])))
    steps = 2
    return pl.pallas_call(
        update,
        grid=(steps,),
        out_shape=(jax.ShapeDtypeStruct((m, k), f32), jax.ShapeDtypeStruct((1, b, n), f32)),
        in_specs=[vmem] * 4,
        out_specs=(
            pl.BlockSpec((m // steps, k), lambda t: (t, 0)),
            pl.BlockSpec((1, b, n), lambda t: (0, 0, 0)),
        ),
        compiler_params=pltpu.CompilerParams(vmem_limit_bytes=16 * 1024 * 1024),
        name="tile_update",
    )(*held)


def solution(mesh):
    return jax.shard_map(
        shards,
        mesh=mesh,
        in_specs=(P("row", "col"), P(None, None, "row"), P()),
        out_specs=(P("row", "col"), P(None, None, "row")),
        check_vma=False,
    )
```

```python
import functools

import jax
import jax.numpy as jnp
from jax import lax
from jax.experimental import pallas as pl
from jax.experimental.pallas import tpu as pltpu
from jax.sharding import PartitionSpec as P

MESH = pl.DeviceIdType.MESH


def split(x):
    hi = x.astype(jnp.bfloat16)
    return hi, (x - hi.astype(jnp.float32)).astype(jnp.bfloat16)


def dot(a, b, da, db):
    return lax.dot_general(a, b, (((da,), (db,)), ((), ())), preferred_element_type=jnp.float32)


def dot3(a, b, da, db):
    ah, al = split(a)
    bh, bl = split(b)
    return dot(ah, bh, da, db) + (dot(ah, bl, da, db) + dot(al, bh, da, db))


def wrap(x, size):
    return jnp.where(x >= size, x - size, x)


def kernel(
    nr, nc, v_hbm, a_hbm, f_hbm, a_ref, left_ref, right_ref, w_ref,
    a_hi, a_lo, v_ref, f_ref, vown, vrecv, pbuf, precv, yown, yrecv, yrow, srow, spart, sown, sfull,
    in_sem, gv_send, gv_recv, rs_send, rs_recv, gy_send, gy_recv, yr_send, yr_recv, sr_send, sr_recv, sc_send, sc_recv,
):
    ratio = nr // nc
    r, c = lax.axis_index("row"), lax.axis_index("col")
    home, i = r // ratio, r % ratio
    at_home = home == c
    n = v_hbm.shape[2]
    b = f_ref.shape[0]
    h2 = b // nc // 2

    v_copy = pltpu.make_async_copy(v_hbm, v_ref, in_sem.at[0])
    a_copy = pltpu.make_async_copy(a_hbm, a_ref, in_sem.at[1])
    f_copy = pltpu.make_async_copy(f_hbm, f_ref, in_sem.at[2])
    v_copy.start()
    f_copy.start()
    a_copy.start()

    def remote(src, dst, send, recv, row, col):
        return pltpu.make_async_remote_copy(
            src_ref=src, dst_ref=dst, send_sem=send, recv_sem=recv, device_id=(row, col), device_id_type=MESH
        )

    row_peers = [wrap(r + k, nr) for k in range(1, nr)]
    col_peers = [wrap(c + k, nc) for k in range(1, nc)]

    def signal(row, col):
        pl.semaphore_signal(barrier, inc=1, device_id=(row, col), device_id_type=MESH)

    barrier = pltpu.get_barrier_semaphore()
    for t in row_peers:
        signal(t, c)
    for q in col_peers:
        signal(r, q)
    for q in col_peers:
        for e in range(ratio):
            signal(c * ratio + e, q)
    pl.semaphore_wait(barrier, nr - 1 + nc - 1 + jnp.where(at_home, 0, nr))

    class Gather:
        def __init__(self, src, buf, send, recv):
            self.src, self.buf, self.send, self.recv = src, buf, send, recv
            self.copies = [
                remote(src, buf.at[i, c], send.at[k], recv.at[i, c], wrap(r + k, nr), home) for k in range(nr)
            ]
            for copy in self.copies[1:]:
                copy.start()
            pl.when(jnp.logical_not(at_home))(self.copies[0].start)

            @pl.when(at_home)
            def _():
                buf[i, c] = src[...]

        def wait(self):
            for j in range(nc):
                q = wrap(c + j, nc)
                for e in range(ratio):
                    arrival = remote(self.src, self.buf.at[e, q], self.send.at[0], self.recv.at[e, q], r, c)
                    if j:
                        arrival.wait_recv()
                    else:
                        pl.when(c * ratio + e != r)(arrival.wait_recv)

        def end(self):
            pl.when(jnp.logical_not(at_home))(self.copies[0].wait_send)
            for copy in self.copies[1:]:
                copy.wait_send()

    def columns(buf, parts):
        return jnp.concatenate(
            [
                jnp.concatenate([buf[m, t, q, :, :n] for q in range(nc) for m in parts], axis=0)
                for t in range(ratio)
            ],
            axis=1,
        )

    v_copy.wait()
    for m in range(2):
        vown[m, :, :n] = v_ref[c, m * h2:(m + 1) * h2]
    gv = [Gather(vown.at[m], vrecv.at[m], gv_send.at[m], gv_recv.at[m]) for m in range(2)]

    f_copy.wait()
    a_copy.wait()
    hi, lo = split(a_ref[...])
    a_hi[...] = hi
    a_lo[...] = lo
    v_rows = jnp.concatenate([v_ref[q] for q in range(nc)], axis=0)

    rs = []
    for m in range(2):
        gv[m].wait()
        vh, vl = split(columns(vrecv, (m,)))
        both = dot(jnp.concatenate([vh, vl], axis=0), a_hi[...], 1, 1)
        partial = both[:b // 2] + (both[b // 2:] + dot(vh, a_lo[...], 1, 1))
        for q in range(nc):
            pbuf[m, q, :, :n] = partial[q * h2:(q + 1) * h2]
        for k, q in enumerate(col_peers):
            copy = remote(pbuf.at[m, q], precv.at[m, c], rs_send.at[m, k], rs_recv.at[m, c], r, q)
            copy.start()
            rs.append(copy)

    v_cols = columns(vrecv, range(2))
    vh, vl = split(v_cols)
    right_ref[b:2 * b] = vh
    right_ref[3 * b:4 * b] = vl
    right_ref[5 * b:] = vh

    gy, yr, own = [], [], []
    for m in range(2):
        total = pbuf[m, c]
        for k, q in enumerate(col_peers):
            remote(pbuf.at[m, q], precv.at[m, q], rs_send.at[m, k], rs_recv.at[m, q], r, q).wait_recv()
            total = total + precv[m, q]
        yown[m] = total
        yrow[m, c] = total
        own.append(total[:, :n])
        gy.append(Gather(yown.at[m], yrecv.at[m], gy_send.at[m], gy_recv.at[m]))
        if m:
            term = dot3(jnp.concatenate(own, axis=0), v_rows, 1, 1)
            spart[:, :b] = term
            srow[r, :, :b] = term
            sr = [remote(spart, srow.at[r], sr_send.at[k], sr_recv.at[r], t, c) for k, t in enumerate(row_peers)]
            for copy in sr:
                copy.start()
        for k, q in enumerate(col_peers):
            copy = remote(yown.at[m], yrow.at[m, c], yr_send.at[m, k], yr_recv.at[m, c], r, q)
            copy.start()
            yr.append(copy)

    for k, t in enumerate(row_peers):
        remote(spart, srow.at[t], sr_send.at[k], sr_recv.at[t], t, c).wait_recv()
    s = srow[0]
    for t in range(1, nr):
        s = s + srow[t]
    sown[...] = s
    sfull[c] = s
    sc = [remote(sown, sfull.at[c], sc_send.at[k], sc_recv.at[c], r, q) for k, q in enumerate(col_peers)]
    for copy in sc:
        copy.start()

    factor = f_ref[...]
    for m in range(2):
        for k, q in enumerate(col_peers):
            remote(yown.at[m], yrow.at[m, q], yr_send.at[m, k], yr_recv.at[m, q], r, q).wait_recv()
    y_rows = jnp.concatenate([yrow[m, q, :, :n] for q in range(nc) for m in range(2)], axis=0)
    x_rows = dot3(factor, y_rows, 0, 0)
    for k, q in enumerate(col_peers):
        remote(sown, sfull.at[q], sc_send.at[k], sc_recv.at[q], r, q).wait_recv()
    square = jnp.concatenate([sfull[q, :, :b] for q in range(nc)], axis=0)
    mixing = 0.5 * dot3(factor, dot3(square, factor, 1, 0), 0, 0)
    w_rows = x_rows - dot3(mixing, v_rows, 1, 0)
    w_ref[0] = w_rows
    lh, ll = split(jnp.concatenate([v_rows, w_rows], axis=0).T)
    left_ref[...] = jnp.concatenate([lh, lh, ll], axis=1)
    mixed = dot3(mixing, v_cols, 1, 0)

    for m in range(2):
        gy[m].wait()
    wh, wl = split(dot3(factor, columns(yrecv, range(2)), 0, 0) - mixed)
    right_ref[:b] = wh
    right_ref[2 * b:3 * b] = wl
    right_ref[4 * b:5 * b] = wh

    for gather in gv + gy:
        gather.end()
    for copy in rs + sr + yr + sc:
        copy.wait_send()


def update(a_ref, left_ref, right_ref, w_ref, out_ref, companion_ref):
    size = out_ref.shape[0]
    rows = pl.ds(pl.multiple_of(pl.program_id(0) * size, size), size)
    out_ref[...] = a_ref[rows, :] - dot(left_ref[rows, :], right_ref[...], 1, 0)

    @pl.when(pl.program_id(0) == 0)
    def _():
        companion_ref[...] = w_ref[...]


def shards(matrix, reflectors, factors):
    nr, nc = lax.axis_size("row"), lax.axis_size("col")
    _, b, n = reflectors.shape
    m, k = matrix.shape
    ratio, h = nr // nc, b // nc
    wide = pl.cdiv(n, 128) * 128
    f32 = jnp.float32
    dma = pltpu.SemaphoreType.DMA
    vmem = pl.BlockSpec(memory_space=pltpu.VMEM)
    hbm = pl.BlockSpec(memory_space=pltpu.HBM)
    held = pl.pallas_call(
        functools.partial(kernel, nr, nc),
        out_shape=(
            jax.ShapeDtypeStruct((m, k), f32),
            jax.ShapeDtypeStruct((m, 6 * b), jnp.bfloat16),
            jax.ShapeDtypeStruct((6 * b, k), jnp.bfloat16),
            jax.ShapeDtypeStruct((1, b, n), f32),
        ),
        in_specs=[hbm, hbm, hbm],
        out_specs=(vmem,) * 4,
        scratch_shapes=[
            pltpu.VMEM((m, k), jnp.bfloat16),
            pltpu.VMEM((m, k), jnp.bfloat16),
            pltpu.VMEM((nc, h, n), f32),
            pltpu.VMEM((b, b), f32),
            pltpu.VMEM((2, h // 2, wide), f32),
            pltpu.VMEM((2, ratio, nc, h // 2, wide), f32),
            pltpu.VMEM((2, nc, h // 2, wide), f32),
            pltpu.VMEM((2, nc, h // 2, wide), f32),
            pltpu.VMEM((2, h // 2, wide), f32),
            pltpu.VMEM((2, ratio, nc, h // 2, wide), f32),
            pltpu.VMEM((2, nc, h // 2, wide), f32),
            pltpu.VMEM((nr, h, 2 * b), f32),
            pltpu.VMEM((h, 2 * b), f32),
            pltpu.VMEM((h, 2 * b), f32),
            pltpu.VMEM((nc, h, 2 * b), f32),
            dma((3,)),
            dma((2, nr)), dma((2, ratio, nc)),
            dma((2, nc - 1)), dma((2, nc)),
            dma((2, nr)), dma((2, ratio, nc)),
            dma((2, nc - 1)), dma((2, nc)),
            dma((nr - 1,)), dma((nr,)),
            dma((nc - 1,)), dma((nc,)),
        ],
        compiler_params=pltpu.CompilerParams(
            collective_id=0, has_side_effects=True, vmem_limit_bytes=32 * 1024 * 1024
        ),
        name="reflector_update",
    )(*(pltpu.with_memory_space_constraint(x, pltpu.HBM) for x in (reflectors.reshape(nc, h, n), matrix, factors[0])))
    steps = 2
    return pl.pallas_call(
        update,
        grid=(steps,),
        out_shape=(jax.ShapeDtypeStruct((m, k), f32), jax.ShapeDtypeStruct((1, b, n), f32)),
        in_specs=[vmem] * 4,
        out_specs=(
            pl.BlockSpec((m // steps, k), lambda t: (t, 0)),
            pl.BlockSpec((1, b, n), lambda t: (0, 0, 0)),
        ),
        compiler_params=pltpu.CompilerParams(vmem_limit_bytes=16 * 1024 * 1024),
        name="tile_update",
    )(*held)


def solution(mesh):
    return jax.shard_map(
        shards,
        mesh=mesh,
        in_specs=(P("row", "col"), P(None, None, "row"), P()),
        out_specs=(P("row", "col"), P(None, None, "row")),
        check_vma=False,
    )
```

```python
import functools

import jax
import jax.numpy as jnp
from jax import lax
from jax.experimental import pallas as pl
from jax.experimental.pallas import tpu as pltpu
from jax.sharding import PartitionSpec as P

MESH = pl.DeviceIdType.MESH


def split(x):
    hi = x.astype(jnp.bfloat16)
    return hi, (x - hi.astype(jnp.float32)).astype(jnp.bfloat16)


def dot(a, b, da, db):
    return lax.dot_general(a, b, (((da,), (db,)), ((), ())), preferred_element_type=jnp.float32)


def dot3(a, b, da, db):
    ah, al = split(a)
    bh, bl = split(b)
    return dot(ah, bh, da, db) + (dot(ah, bl, da, db) + dot(al, bh, da, db))


def wrap(x, size):
    return jnp.where(x >= size, x - size, x)


def kernel(
    nr, nc, v_hbm, a_hbm, f_hbm, a_ref, left_ref, right_ref, w_ref,
    a_hi, a_lo, v_ref, f_ref, vrecv, pbuf, precv, yown, yrecv, yrow, srow, spart, sown, sfull,
    in_sem, gv_send, gv_recv, rs_send, rs_recv, gy_send, gy_recv, yr_send, yr_recv, sr_send, sr_recv, sc_send, sc_recv,
):
    ratio = nr // nc
    r, c = lax.axis_index("row"), lax.axis_index("col")
    home, i = r // ratio, r % ratio
    at_home = home == c
    n = v_hbm.shape[2]
    b = f_ref.shape[0]
    h = b // nc

    v_copy = pltpu.make_async_copy(v_hbm, v_ref, in_sem.at[0])
    a_copy = pltpu.make_async_copy(a_hbm, a_ref, in_sem.at[1])
    f_copy = pltpu.make_async_copy(f_hbm, f_ref, in_sem.at[2])
    v_copy.start()
    f_copy.start()
    a_copy.start()

    def remote(src, dst, send, recv, row, col):
        return pltpu.make_async_remote_copy(
            src_ref=src, dst_ref=dst, send_sem=send, recv_sem=recv, device_id=(row, col), device_id_type=MESH
        )

    row_peers = [wrap(r + k, nr) for k in range(1, nr)]
    col_peers = [wrap(c + k, nc) for k in range(1, nc)]

    def signal(row, col):
        pl.semaphore_signal(barrier, inc=1, device_id=(row, col), device_id_type=MESH)

    barrier = pltpu.get_barrier_semaphore()
    for t in row_peers:
        signal(t, c)
    for q in col_peers:
        signal(r, q)
    for q in col_peers:
        for e in range(ratio):
            signal(c * ratio + e, q)
    pl.semaphore_wait(barrier, nr - 1 + nc - 1 + jnp.where(at_home, 0, nr))

    class Gather:
        def __init__(self, src, buf, send, recv):
            self.src, self.buf, self.send, self.recv = src, buf, send, recv
            self.copies = [
                remote(src, buf.at[i, c], send.at[k], recv.at[i, c], wrap(r + k, nr), home) for k in range(nr)
            ]
            for copy in self.copies[1:]:
                copy.start()
            pl.when(jnp.logical_not(at_home))(self.copies[0].start)

            @pl.when(at_home)
            def _():
                buf[i, c] = src[...]

        def wait(self):
            for j in range(nc):
                q = wrap(c + j, nc)
                for e in range(ratio):
                    arrival = remote(self.src, self.buf.at[e, q], self.send.at[0], self.recv.at[e, q], r, c)
                    if j:
                        arrival.wait_recv()
                    else:
                        pl.when(c * ratio + e != r)(arrival.wait_recv)

        def end(self):
            pl.when(jnp.logical_not(at_home))(self.copies[0].wait_send)
            for copy in self.copies[1:]:
                copy.wait_send()

    def columns(buf):
        return jnp.concatenate(
            [jnp.concatenate([buf[t, q, :, :n] for q in range(nc)], axis=0) for t in range(ratio)], axis=1
        )

    def unless(own, action):
        pl.when(jnp.logical_not(own))(action)

    v_copy.wait()
    gv = []
    for e in range(ratio):
        t = c + e * nc
        copy = remote(v_ref, vrecv.at[i], gv_send.at[e], gv_recv.at[i], t, home)
        own = jnp.logical_and(at_home, t == r)
        unless(own, copy.start)
        gv.append((own, copy))

        @pl.when(own)
        def _():
            vrecv[i] = v_ref[...]

    f_copy.wait()
    a_copy.wait()
    hi, lo = split(a_ref[...])
    a_hi[...] = hi
    a_lo[...] = lo
    v_rows = jnp.concatenate([v_ref[q] for q in range(nc)], axis=0)
    rh, rl = split(v_rows.T)

    helper = lax.rem(r, nc)
    for e in range(ratio):
        own = jnp.logical_and(c * ratio + e == r, helper == c)
        unless(own, remote(v_ref, vrecv.at[e], gv_send.at[e], gv_recv.at[e], c * ratio + e, helper).wait_recv)
    v_cols = columns(vrecv)
    vh, vl = split(v_cols)
    both = dot(jnp.concatenate([vh, vl], axis=0), a_hi[...], 1, 1)
    partial = both[:b] + (both[b:] + dot(vh, a_lo[...], 1, 1))
    for q in range(nc):
        pbuf[q, :, :n] = partial[q * h:(q + 1) * h]

    rs = [remote(pbuf.at[q], precv.at[c], rs_send.at[k], rs_recv.at[c], r, q) for k, q in enumerate(col_peers)]
    for copy in rs:
        copy.start()
    right_ref[b:2 * b] = vh
    right_ref[3 * b:4 * b] = vl
    right_ref[5 * b:] = vh
    left_ref[:, :b] = rh
    left_ref[:, 2 * b:3 * b] = rh
    left_ref[:, 4 * b:5 * b] = rl
    total = pbuf[c]
    for k, q in enumerate(col_peers):
        remote(pbuf.at[q], precv.at[q], rs_send.at[k], rs_recv.at[q], r, q).wait_recv()
        total = total + precv[q]
    yown[...] = total
    term = dot3(total[:, :n], v_rows, 1, 1)
    spart[:, :b] = term
    srow[r, :, :b] = term

    sr = [remote(spart, srow.at[r], sr_send.at[k], sr_recv.at[r], t, c) for k, t in enumerate(row_peers)]
    for copy in sr:
        copy.start()
    gy = Gather(yown, yrecv, gy_send, gy_recv)
    yr = [remote(yown, yrow.at[c], yr_send.at[k], yr_recv.at[c], r, q) for k, q in enumerate(col_peers)]
    for copy in yr:
        copy.start()
    yrow[c] = yown[...]

    for k, t in enumerate(row_peers):
        remote(spart, srow.at[t], sr_send.at[k], sr_recv.at[t], t, c).wait_recv()
    s = srow[0]
    for t in range(1, nr):
        s = s + srow[t]
    sown[...] = s
    sfull[c] = s
    sc = [remote(sown, sfull.at[c], sc_send.at[k], sc_recv.at[c], r, q) for k, q in enumerate(col_peers)]
    for copy in sc:
        copy.start()

    factor = f_ref[...]
    for k, q in enumerate(col_peers):
        remote(yown, yrow.at[q], yr_send.at[k], yr_recv.at[q], r, q).wait_recv()
    y_rows = jnp.concatenate([yrow[q, :, :n] for q in range(nc)], axis=0)
    x_rows = dot3(factor, y_rows, 0, 0)
    for k, q in enumerate(col_peers):
        remote(sown, sfull.at[q], sc_send.at[k], sc_recv.at[q], r, q).wait_recv()
    square = jnp.concatenate([sfull[q, :, :b] for q in range(nc)], axis=0)
    mixing = 0.5 * dot3(factor, dot3(square, factor, 1, 0), 0, 0)
    w_rows = x_rows - dot3(mixing, v_rows, 1, 0)
    w_ref[0] = w_rows
    lh, ll = split(w_rows.T)
    left_ref[:, b:2 * b] = lh
    left_ref[:, 3 * b:4 * b] = lh
    left_ref[:, 5 * b:] = ll
    mixed = dot3(mixing, v_cols, 1, 0)
    for own, copy in gv:
        unless(own, copy.wait_send)
    gy.end()
    for copy in rs + sr + yr + sc:
        copy.wait_send()

    gy.wait()
    wh, wl = split(dot3(factor, columns(yrecv), 0, 0) - mixed)
    right_ref[:b] = wh
    right_ref[2 * b:3 * b] = wl
    right_ref[4 * b:5 * b] = wh


def update(a_ref, left_ref, right_ref, w_ref, out_ref, companion_ref):
    size = out_ref.shape[0]
    rows = pl.ds(pl.multiple_of(pl.program_id(0) * size, size), size)
    out_ref[...] = a_ref[rows, :] - dot(left_ref[rows, :], right_ref[...], 1, 0)

    @pl.when(pl.program_id(0) == 0)
    def _():
        companion_ref[...] = w_ref[...]


def shards(matrix, reflectors, factors):
    nr, nc = lax.axis_size("row"), lax.axis_size("col")
    _, b, n = reflectors.shape
    m, k = matrix.shape
    ratio, h = nr // nc, b // nc
    wide = pl.cdiv(n, 128) * 128
    f32 = jnp.float32
    dma = pltpu.SemaphoreType.DMA
    vmem = pl.BlockSpec(memory_space=pltpu.VMEM)
    hbm = pl.BlockSpec(memory_space=pltpu.HBM)
    held = pl.pallas_call(
        functools.partial(kernel, nr, nc),
        out_shape=(
            jax.ShapeDtypeStruct((m, k), f32),
            jax.ShapeDtypeStruct((m, 6 * b), jnp.bfloat16),
            jax.ShapeDtypeStruct((6 * b, k), jnp.bfloat16),
            jax.ShapeDtypeStruct((1, b, n), f32),
        ),
        in_specs=[hbm, hbm, hbm],
        out_specs=(vmem,) * 4,
        scratch_shapes=[
            pltpu.VMEM((m, k), jnp.bfloat16),
            pltpu.VMEM((m, k), jnp.bfloat16),
            pltpu.VMEM((nc, h, n), f32),
            pltpu.VMEM((b, b), f32),
            pltpu.VMEM((ratio, nc, h, n), f32),
            pltpu.VMEM((nc, h, wide), f32),
            pltpu.VMEM((nc, h, wide), f32),
            pltpu.VMEM((h, wide), f32),
            pltpu.VMEM((ratio, nc, h, wide), f32),
            pltpu.VMEM((nc, h, wide), f32),
            pltpu.VMEM((nr, h, 2 * b), f32),
            pltpu.VMEM((h, 2 * b), f32),
            pltpu.VMEM((h, 2 * b), f32),
            pltpu.VMEM((nc, h, 2 * b), f32),
            dma((3,)),
            dma((ratio,)), dma((ratio,)),
            dma((nc - 1,)), dma((nc,)),
            dma((nr,)), dma((ratio, nc)),
            dma((nc - 1,)), dma((nc,)),
            dma((nr - 1,)), dma((nr,)),
            dma((nc - 1,)), dma((nc,)),
        ],
        compiler_params=pltpu.CompilerParams(
            collective_id=0, has_side_effects=True, vmem_limit_bytes=32 * 1024 * 1024
        ),
        name="reflector_update",
    )(*(pltpu.with_memory_space_constraint(x, pltpu.HBM) for x in (reflectors.reshape(nc, h, n), matrix, factors[0])))
    steps = 2
    return pl.pallas_call(
        update,
        grid=(steps,),
        out_shape=(jax.ShapeDtypeStruct((m, k), f32), jax.ShapeDtypeStruct((1, b, n), f32)),
        in_specs=[vmem] * 4,
        out_specs=(
            pl.BlockSpec((m // steps, k), lambda t: (t, 0)),
            pl.BlockSpec((1, b, n), lambda t: (0, 0, 0)),
        ),
        compiler_params=pltpu.CompilerParams(vmem_limit_bytes=16 * 1024 * 1024),
        name="tile_update",
    )(*held)


def solution(mesh):
    return jax.shard_map(
        shards,
        mesh=mesh,
        in_specs=(P("row", "col"), P(None, None, "row"), P()),
        out_specs=(P("row", "col"), P(None, None, "row")),
        check_vma=False,
    )
```

```python
import functools

import jax
import jax.numpy as jnp
from jax import lax
from jax.experimental import pallas as pl
from jax.experimental.pallas import tpu as pltpu
from jax.sharding import PartitionSpec as P

MESH = pl.DeviceIdType.MESH


def split(x):
    hi = x.astype(jnp.bfloat16)
    return hi, (x - hi.astype(jnp.float32)).astype(jnp.bfloat16)


def dot(a, b, da, db):
    return lax.dot_general(a, b, (((da,), (db,)), ((), ())), preferred_element_type=jnp.float32)


def dot3(a, b, da, db):
    ah, al = split(a)
    bh, bl = split(b)
    return dot(ah, bh, da, db) + (dot(ah, bl, da, db) + dot(al, bh, da, db))


def wrap(x, size):
    return jnp.where(x >= size, x - size, x)


def kernel(
    nr, nc, v_hbm, a_hbm, f_hbm, a_ref, left_ref, right_ref, w_ref,
    a_hi, a_lo, v_ref, f_ref, vrecv, pbuf, precv, yown, yrecv, yrow, srow, spart, sown, sfull,
    in_sem, gv_send, gv_recv, rs_send, rs_recv, gy_send, gy_recv, yr_send, yr_recv, sr_send, sr_recv, sc_send, sc_recv,
):
    ratio = nr // nc
    r, c = lax.axis_index("row"), lax.axis_index("col")
    home, i = r // ratio, r % ratio
    at_home = home == c
    n = v_hbm.shape[2]
    b = f_ref.shape[0]
    h = b // nc

    v_copy = pltpu.make_async_copy(v_hbm, v_ref, in_sem.at[0])
    a_copy = pltpu.make_async_copy(a_hbm, a_ref, in_sem.at[1])
    f_copy = pltpu.make_async_copy(f_hbm, f_ref, in_sem.at[2])
    v_copy.start()
    f_copy.start()
    a_copy.start()

    def remote(src, dst, send, recv, row, col):
        return pltpu.make_async_remote_copy(
            src_ref=src, dst_ref=dst, send_sem=send, recv_sem=recv, device_id=(row, col), device_id_type=MESH
        )

    row_peers = [wrap(r + k, nr) for k in range(1, nr)]
    col_peers = [wrap(c + k, nc) for k in range(1, nc)]

    def signal(row, col):
        pl.semaphore_signal(barrier, inc=1, device_id=(row, col), device_id_type=MESH)

    barrier = pltpu.get_barrier_semaphore()
    for t in row_peers:
        signal(t, c)
    for q in col_peers:
        signal(r, q)
    for q in col_peers:
        for e in range(ratio):
            signal(c * ratio + e, q)
    pl.semaphore_wait(barrier, nr - 1 + nc - 1 + jnp.where(at_home, 0, nr))

    class Gather:
        def __init__(self, src, buf, send, recv):
            self.src, self.buf, self.send, self.recv = src, buf, send, recv
            self.copies = [
                remote(src, buf.at[i, c], send.at[k], recv.at[i, c], wrap(r + k, nr), home) for k in range(nr)
            ]
            for copy in self.copies[1:]:
                copy.start()
            pl.when(jnp.logical_not(at_home))(self.copies[0].start)

            @pl.when(at_home)
            def _():
                buf[i, c] = src[...]

        def wait(self):
            for j in range(nc):
                q = wrap(c + j, nc)
                for e in range(ratio):
                    arrival = remote(self.src, self.buf.at[e, q], self.send.at[0], self.recv.at[e, q], r, c)
                    if j:
                        arrival.wait_recv()
                    else:
                        pl.when(c * ratio + e != r)(arrival.wait_recv)

        def end(self):
            pl.when(jnp.logical_not(at_home))(self.copies[0].wait_send)
            for copy in self.copies[1:]:
                copy.wait_send()

    def columns(buf):
        return jnp.concatenate(
            [jnp.concatenate([buf[t, q, :, :n] for q in range(nc)], axis=0) for t in range(ratio)], axis=1
        )

    def unless(own, action):
        pl.when(jnp.logical_not(own))(action)

    v_copy.wait()
    gv = []
    for e in range(ratio):
        t = c + e * nc
        copy = remote(v_ref, vrecv.at[i], gv_send.at[e], gv_recv.at[i], t, home)
        own = jnp.logical_and(at_home, t == r)
        unless(own, copy.start)
        gv.append((own, copy))

        @pl.when(own)
        def _():
            vrecv[i] = v_ref[...]

    f_copy.wait()
    a_copy.wait()
    hi, lo = split(a_ref[...].T)
    a_hi[...] = hi
    a_lo[...] = lo
    v_rows = jnp.concatenate([v_ref[q] for q in range(nc)], axis=0)
    rh, rl = split(v_rows.T)

    helper = lax.rem(r, nc)
    for e in range(ratio):
        own = jnp.logical_and(c * ratio + e == r, helper == c)
        unless(own, remote(v_ref, vrecv.at[e], gv_send.at[e], gv_recv.at[e], c * ratio + e, helper).wait_recv)
    v_cols = columns(vrecv)
    vh, vl = split(v_cols)
    both = dot(jnp.concatenate([vh, vl], axis=0), a_hi[...], 1, 0)
    partial = both[:b] + (both[b:] + dot(vh, a_lo[...], 1, 0))
    for q in range(nc):
        pbuf[q, :, :n] = partial[q * h:(q + 1) * h]

    rs = [remote(pbuf.at[q], precv.at[c], rs_send.at[k], rs_recv.at[c], r, q) for k, q in enumerate(col_peers)]
    for copy in rs:
        copy.start()
    right_ref[b:2 * b] = vh
    right_ref[3 * b:4 * b] = vl
    right_ref[5 * b:] = vh
    left_ref[:, :b] = rh
    left_ref[:, 2 * b:3 * b] = rh
    left_ref[:, 4 * b:5 * b] = rl
    total = pbuf[c]
    for k, q in enumerate(col_peers):
        remote(pbuf.at[q], precv.at[q], rs_send.at[k], rs_recv.at[q], r, q).wait_recv()
        total = total + precv[q]
    yown[...] = total
    term = dot3(total[:, :n], v_rows, 1, 1)
    spart[:, :b] = term
    srow[r, :, :b] = term

    sr = [remote(spart, srow.at[r], sr_send.at[k], sr_recv.at[r], t, c) for k, t in enumerate(row_peers)]
    for copy in sr:
        copy.start()
    gy = Gather(yown, yrecv, gy_send, gy_recv)
    yr = [remote(yown, yrow.at[c], yr_send.at[k], yr_recv.at[c], r, q) for k, q in enumerate(col_peers)]
    for copy in yr:
        copy.start()
    yrow[c] = yown[...]

    for k, t in enumerate(row_peers):
        remote(spart, srow.at[t], sr_send.at[k], sr_recv.at[t], t, c).wait_recv()
    s = srow[0]
    for t in range(1, nr):
        s = s + srow[t]
    sown[...] = s
    sfull[c] = s
    sc = [remote(sown, sfull.at[c], sc_send.at[k], sc_recv.at[c], r, q) for k, q in enumerate(col_peers)]
    for copy in sc:
        copy.start()

    factor = f_ref[...]
    for k, q in enumerate(col_peers):
        remote(yown, yrow.at[q], yr_send.at[k], yr_recv.at[q], r, q).wait_recv()
    y_rows = jnp.concatenate([yrow[q, :, :n] for q in range(nc)], axis=0)
    x_rows = dot3(factor, y_rows, 0, 0)
    for k, q in enumerate(col_peers):
        remote(sown, sfull.at[q], sc_send.at[k], sc_recv.at[q], r, q).wait_recv()
    square = jnp.concatenate([sfull[q, :, :b] for q in range(nc)], axis=0)
    mixing = 0.5 * dot3(factor, dot3(square, factor, 1, 0), 0, 0)
    w_rows = x_rows - dot3(mixing, v_rows, 1, 0)
    w_ref[0] = w_rows
    lh, ll = split(w_rows.T)
    left_ref[:, b:2 * b] = lh
    left_ref[:, 3 * b:4 * b] = lh
    left_ref[:, 5 * b:] = ll
    mixed = dot3(mixing, v_cols, 1, 0)
    for own, copy in gv:
        unless(own, copy.wait_send)
    gy.end()
    for copy in rs + sr + yr + sc:
        copy.wait_send()

    gy.wait()
    wh, wl = split(dot3(factor, columns(yrecv), 0, 0) - mixed)
    right_ref[:b] = wh
    right_ref[2 * b:3 * b] = wl
    right_ref[4 * b:5 * b] = wh


def update(a_ref, left_ref, right_ref, w_ref, out_ref, companion_ref):
    size = out_ref.shape[0]
    rows = pl.ds(pl.multiple_of(pl.program_id(0) * size, size), size)
    out_ref[...] = a_ref[rows, :] - dot(left_ref[rows, :], right_ref[...], 1, 0)

    @pl.when(pl.program_id(0) == 0)
    def _():
        companion_ref[...] = w_ref[...]


def shards(matrix, reflectors, factors):
    nr, nc = lax.axis_size("row"), lax.axis_size("col")
    _, b, n = reflectors.shape
    m, k = matrix.shape
    ratio, h = nr // nc, b // nc
    wide = pl.cdiv(n, 128) * 128
    f32 = jnp.float32
    dma = pltpu.SemaphoreType.DMA
    vmem = pl.BlockSpec(memory_space=pltpu.VMEM)
    hbm = pl.BlockSpec(memory_space=pltpu.HBM)
    held = pl.pallas_call(
        functools.partial(kernel, nr, nc),
        out_shape=(
            jax.ShapeDtypeStruct((m, k), f32),
            jax.ShapeDtypeStruct((m, 6 * b), jnp.bfloat16),
            jax.ShapeDtypeStruct((6 * b, k), jnp.bfloat16),
            jax.ShapeDtypeStruct((1, b, n), f32),
        ),
        in_specs=[hbm, hbm, hbm],
        out_specs=(vmem,) * 4,
        scratch_shapes=[
            pltpu.VMEM((k, m), jnp.bfloat16),
            pltpu.VMEM((k, m), jnp.bfloat16),
            pltpu.VMEM((nc, h, n), f32),
            pltpu.VMEM((b, b), f32),
            pltpu.VMEM((ratio, nc, h, n), f32),
            pltpu.VMEM((nc, h, wide), f32),
            pltpu.VMEM((nc, h, wide), f32),
            pltpu.VMEM((h, wide), f32),
            pltpu.VMEM((ratio, nc, h, wide), f32),
            pltpu.VMEM((nc, h, wide), f32),
            pltpu.VMEM((nr, h, 2 * b), f32),
            pltpu.VMEM((h, 2 * b), f32),
            pltpu.VMEM((h, 2 * b), f32),
            pltpu.VMEM((nc, h, 2 * b), f32),
            dma((3,)),
            dma((ratio,)), dma((ratio,)),
            dma((nc - 1,)), dma((nc,)),
            dma((nr,)), dma((ratio, nc)),
            dma((nc - 1,)), dma((nc,)),
            dma((nr - 1,)), dma((nr,)),
            dma((nc - 1,)), dma((nc,)),
        ],
        compiler_params=pltpu.CompilerParams(
            collective_id=0, has_side_effects=True, vmem_limit_bytes=32 * 1024 * 1024
        ),
        name="reflector_update",
    )(*(pltpu.with_memory_space_constraint(x, pltpu.HBM) for x in (reflectors.reshape(nc, h, n), matrix, factors[0])))
    steps = 2
    return pl.pallas_call(
        update,
        grid=(steps,),
        out_shape=(jax.ShapeDtypeStruct((m, k), f32), jax.ShapeDtypeStruct((1, b, n), f32)),
        in_specs=[vmem] * 4,
        out_specs=(
            pl.BlockSpec((m // steps, k), lambda t: (t, 0)),
            pl.BlockSpec((1, b, n), lambda t: (0, 0, 0)),
        ),
        compiler_params=pltpu.CompilerParams(vmem_limit_bytes=16 * 1024 * 1024),
        name="tile_update",
    )(*held)


def solution(mesh):
    return jax.shard_map(
        shards,
        mesh=mesh,
        in_specs=(P("row", "col"), P(None, None, "row"), P()),
        out_specs=(P("row", "col"), P(None, None, "row")),
        check_vma=False,
    )
```

```python
import functools

import jax
import jax.numpy as jnp
from jax import lax
from jax.experimental import pallas as pl
from jax.experimental.pallas import tpu as pltpu
from jax.sharding import PartitionSpec as P

MESH = pl.DeviceIdType.MESH


def split(x):
    hi = x.astype(jnp.bfloat16)
    return hi, (x - hi.astype(jnp.float32)).astype(jnp.bfloat16)


def dot(a, b, da, db):
    return lax.dot_general(a, b, (((da,), (db,)), ((), ())), preferred_element_type=jnp.float32)


def dot3(a, b, da, db):
    ah, al = split(a)
    bh, bl = split(b)
    return dot(ah, bh, da, db) + (dot(ah, bl, da, db) + dot(al, bh, da, db))


def wrap(x, size):
    return jnp.where(x >= size, x - size, x)


def kernel(
    nr, nc, v_hbm, a_hbm, f_hbm, a_ref, left_ref, right_ref, w_ref,
    a_hi, a_lo, v_ref, f_ref, vrecv, pbuf, precv, yown, yrecv, yrow, srow, spart, sown, sfull,
    in_sem, gv_send, gv_recv, rs_send, rs_recv, gy_send, gy_recv, yr_send, yr_recv, sr_send, sr_recv, sc_send, sc_recv,
):
    ratio = nr // nc
    r, c = lax.axis_index("row"), lax.axis_index("col")
    home, i = r // ratio, r % ratio
    at_home = home == c
    n = v_hbm.shape[2]
    b = f_ref.shape[0]
    h = b // nc

    v_copy = pltpu.make_async_copy(v_hbm, v_ref, in_sem.at[0])
    a_copy = pltpu.make_async_copy(a_hbm, a_ref, in_sem.at[1])
    f_copy = pltpu.make_async_copy(f_hbm, f_ref, in_sem.at[2])
    v_copy.start()
    f_copy.start()
    a_copy.start()

    def remote(src, dst, send, recv, row, col):
        return pltpu.make_async_remote_copy(
            src_ref=src, dst_ref=dst, send_sem=send, recv_sem=recv, device_id=(row, col), device_id_type=MESH
        )

    row_peers = [wrap(r + k, nr) for k in range(1, nr)]
    col_peers = [wrap(c + k, nc) for k in range(1, nc)]

    def signal(row, col):
        pl.semaphore_signal(barrier, inc=1, device_id=(row, col), device_id_type=MESH)

    barrier = pltpu.get_barrier_semaphore()
    for t in row_peers:
        signal(t, c)
    for q in col_peers:
        signal(r, q)
    for q in col_peers:
        for e in range(ratio):
            signal(c * ratio + e, q)
    pl.semaphore_wait(barrier, nr - 1 + nc - 1 + jnp.where(at_home, 0, nr))

    class Gather:
        def __init__(self, src, buf, send, recv):
            self.src, self.buf, self.send, self.recv = src, buf, send, recv
            self.copies = [
                remote(src, buf.at[i, c], send.at[k], recv.at[i, c], wrap(r + k, nr), home) for k in range(nr)
            ]
            for copy in self.copies[1:]:
                copy.start()
            pl.when(jnp.logical_not(at_home))(self.copies[0].start)

            @pl.when(at_home)
            def _():
                buf[i, c] = src[...]

        def wait(self):
            for j in range(nc):
                q = wrap(c + j, nc)
                for e in range(ratio):
                    arrival = remote(self.src, self.buf.at[e, q], self.send.at[0], self.recv.at[e, q], r, c)
                    if j:
                        arrival.wait_recv()
                    else:
                        pl.when(c * ratio + e != r)(arrival.wait_recv)

        def end(self):
            pl.when(jnp.logical_not(at_home))(self.copies[0].wait_send)
            for copy in self.copies[1:]:
                copy.wait_send()

    def columns(buf):
        return jnp.concatenate(
            [jnp.concatenate([buf[t, q, :, :n] for q in range(nc)], axis=0) for t in range(ratio)], axis=1
        )

    def unless(own, action):
        pl.when(jnp.logical_not(own))(action)

    v_copy.wait()
    gv = []
    for e in range(ratio):
        t = c + e * nc
        copy = remote(v_ref, vrecv.at[i], gv_send.at[e], gv_recv.at[i], t, home)
        own = jnp.logical_and(at_home, t == r)
        unless(own, copy.start)
        gv.append((own, copy))

        @pl.when(own)
        def _():
            vrecv[i] = v_ref[...]

    f_copy.wait()
    a_copy.wait()
    hi, lo = split(a_ref[...].T)
    a_hi[...] = hi
    a_lo[...] = lo
    v_rows = jnp.concatenate([v_ref[q] for q in range(nc)], axis=0)
    rh, rl = split(v_rows.T)

    helper = lax.rem(r, nc)
    for e in range(ratio):
        own = jnp.logical_and(c * ratio + e == r, helper == c)
        unless(own, remote(v_ref, vrecv.at[e], gv_send.at[e], gv_recv.at[e], c * ratio + e, helper).wait_recv)
    v_cols = columns(vrecv)
    vh, vl = split(v_cols)
    both = dot(jnp.concatenate([vh, vl], axis=0), a_hi[...], 1, 0)
    partial = both[:b] + (both[b:] + dot(vh, a_lo[...], 1, 0))
    for q in range(nc):
        pbuf[q, :, :n] = partial[q * h:(q + 1) * h]

    rs = [remote(pbuf.at[q], precv.at[c], rs_send.at[k], rs_recv.at[c], r, q) for k, q in enumerate(col_peers)]
    for copy in rs:
        copy.start()
    right_ref[b:2 * b] = vh
    right_ref[3 * b:4 * b] = vl
    right_ref[5 * b:] = vh
    left_ref[:, :b] = rh
    left_ref[:, 2 * b:3 * b] = rh
    left_ref[:, 4 * b:5 * b] = rl
    total = pbuf[c]
    for k, q in enumerate(col_peers):
        remote(pbuf.at[q], precv.at[q], rs_send.at[k], rs_recv.at[q], r, q).wait_recv()
        total = total + precv[q]
    yown[...] = total
    term = dot3(total[:, :n], v_rows, 1, 1)
    spart[:, :b] = term
    srow[r, :, :b] = term

    sr = [remote(spart, srow.at[r], sr_send.at[k], sr_recv.at[r], t, c) for k, t in enumerate(row_peers)]
    for copy in sr:
        copy.start()
    gy = Gather(yown, yrecv, gy_send, gy_recv)
    yr = [remote(yown, yrow.at[c], yr_send.at[k], yr_recv.at[c], r, q) for k, q in enumerate(col_peers)]
    for copy in yr:
        copy.start()
    yrow[c] = yown[...]

    for k, t in enumerate(row_peers):
        remote(spart, srow.at[t], sr_send.at[k], sr_recv.at[t], t, c).wait_recv()
    s = srow[0]
    for t in range(1, nr):
        s = s + srow[t]
    sown[...] = s
    sfull[c] = s
    sc = [remote(sown, sfull.at[c], sc_send.at[k], sc_recv.at[c], r, q) for k, q in enumerate(col_peers)]
    for copy in sc:
        copy.start()

    factor = f_ref[...]
    for k, q in enumerate(col_peers):
        remote(yown, yrow.at[q], yr_send.at[k], yr_recv.at[q], r, q).wait_recv()
    y_rows = jnp.concatenate([yrow[q, :, :n] for q in range(nc)], axis=0)
    x_rows = dot3(factor, y_rows, 0, 0)
    for k, q in enumerate(col_peers):
        remote(sown, sfull.at[q], sc_send.at[k], sc_recv.at[q], r, q).wait_recv()
    square = jnp.concatenate([sfull[q, :, :b] for q in range(nc)], axis=0)
    mixing = 0.5 * dot3(factor, dot3(square, factor, 1, 0), 0, 0)
    w_rows = x_rows - dot3(mixing, v_rows, 1, 0)
    w_ref[0] = w_rows
    lh, ll = split(w_rows.T)
    left_ref[:, b:2 * b] = lh
    left_ref[:, 3 * b:4 * b] = lh
    left_ref[:, 5 * b:] = ll
    mixed = dot3(mixing, v_cols, 1, 0)
    for own, copy in gv:
        unless(own, copy.wait_send)
    gy.end()
    for copy in rs + sr + yr + sc:
        copy.wait_send()

    gy.wait()
    wh, wl = split(dot3(factor, columns(yrecv), 0, 0) - mixed)
    right_ref[:b] = wh
    right_ref[2 * b:3 * b] = wl
    right_ref[4 * b:5 * b] = wh


def update(a_ref, left_ref, right_ref, w_ref, out_ref, companion_ref):
    size = out_ref.shape[0]
    rows = pl.ds(pl.multiple_of(pl.program_id(0) * size, size), size)
    out_ref[...] = a_ref[rows, :] - dot(left_ref[rows, :], right_ref[...], 1, 0)

    @pl.when(pl.program_id(0) == 0)
    def _():
        companion_ref[...] = w_ref[...]


def shards(matrix, reflectors, factors):
    nr, nc = lax.axis_size("row"), lax.axis_size("col")
    _, b, n = reflectors.shape
    m, k = matrix.shape
    ratio, h = nr // nc, b // nc
    wide = pl.cdiv(n, 128) * 128
    f32 = jnp.float32
    dma = pltpu.SemaphoreType.DMA
    vmem = pl.BlockSpec(memory_space=pltpu.VMEM)
    hbm = pl.BlockSpec(memory_space=pltpu.HBM)
    held = pl.pallas_call(
        functools.partial(kernel, nr, nc),
        out_shape=(
            jax.ShapeDtypeStruct((m, k), f32),
            jax.ShapeDtypeStruct((m, 6 * b), jnp.bfloat16),
            jax.ShapeDtypeStruct((6 * b, k), jnp.bfloat16),
            jax.ShapeDtypeStruct((1, b, n), f32),
        ),
        in_specs=[hbm, hbm, hbm],
        out_specs=(vmem,) * 4,
        scratch_shapes=[
            pltpu.VMEM((k, m), jnp.bfloat16),
            pltpu.VMEM((k, m), jnp.bfloat16),
            pltpu.VMEM((nc, h, n), f32),
            pltpu.VMEM((b, b), f32),
            pltpu.VMEM((ratio, nc, h, n), f32),
            pltpu.VMEM((nc, h, wide), f32),
            pltpu.VMEM((nc, h, wide), f32),
            pltpu.VMEM((h, wide), f32),
            pltpu.VMEM((ratio, nc, h, wide), f32),
            pltpu.VMEM((nc, h, wide), f32),
            pltpu.VMEM((nr, h, 2 * b), f32),
            pltpu.VMEM((h, 2 * b), f32),
            pltpu.VMEM((h, 2 * b), f32),
            pltpu.VMEM((nc, h, 2 * b), f32),
            dma((3,)),
            dma((ratio,)), dma((ratio,)),
            dma((nc - 1,)), dma((nc,)),
            dma((nr,)), dma((ratio, nc)),
            dma((nc - 1,)), dma((nc,)),
            dma((nr - 1,)), dma((nr,)),
            dma((nc - 1,)), dma((nc,)),
        ],
        compiler_params=pltpu.CompilerParams(
            collective_id=0, has_side_effects=True, vmem_limit_bytes=32 * 1024 * 1024
        ),
        name="reflector_update",
    )(*(pltpu.with_memory_space_constraint(x, pltpu.HBM) for x in (reflectors.reshape(nc, h, n), matrix, factors[0])))
    steps = 1
    return pl.pallas_call(
        update,
        grid=(steps,),
        out_shape=(jax.ShapeDtypeStruct((m, k), f32), jax.ShapeDtypeStruct((1, b, n), f32)),
        in_specs=[vmem] * 4,
        out_specs=(
            pl.BlockSpec((m // steps, k), lambda t: (t, 0)),
            pl.BlockSpec((1, b, n), lambda t: (0, 0, 0)),
        ),
        compiler_params=pltpu.CompilerParams(vmem_limit_bytes=16 * 1024 * 1024),
        name="tile_update",
    )(*held)


def solution(mesh):
    return jax.shard_map(
        shards,
        mesh=mesh,
        in_specs=(P("row", "col"), P(None, None, "row"), P()),
        out_specs=(P("row", "col"), P(None, None, "row")),
        check_vma=False,
    )
```
